128 devices in a mesh: space: 16 (over z, y), filt: 8 (over x, core).
Axes of the slice: x: 4, y: 4, z: 4, core: 2. Of those that a mesh axis runs over, the one named last changes fastest.
Arguments:
- volume: bfloat16 [16, 32, 4, 64, 256], P(None, 'space'), may hold values from -6 to 6
- weight_first: bfloat16 [27, 128, 64], P(None, 'filt'), may hold values from -0.15625 to 0.15625
- weight_second: bfloat16 [27, 256, 128], P(None, 'filt'), may hold values from -0.109375 to 0.109375
- cotangent: bfloat16 [16, 16, 2, 256, 128], P('space', None, None, 'filt'), may hold values from -0.09375 to 0.09375
Outputs:
- grad_first: float32 [27, 128, 64], P(None, 'filt')
- grad_second: float32 [27, 256, 128], P(None, 'filt')
The draws below stay inside these ranges and needn't reach their ends.
All inputs are finite; a program needn't handle non-finite values.
Results may differ from the reference program's by a relative error of at most 0.0045.
Values may be sent and summed in bfloat16 or wider, within the bound.
No kernel may reach another device: no remote copies, remote signals or barrier semaphores. Data moves between devices by JAX's collectives and lax.ppermute only.
A program may use at most 384 MiB of HBM per device.

```python
import jax
import jax.numpy as jnp

CA = 64
CB = 128
CC = 256
Y = 4
XW = 256
S = 16
Z = 32


def levels(rng, dims, cuts, low, high):
    level = 1.0
    for dim, blocks in cuts:
        heights = jax.random.uniform(jax.random.fold_in(jax.random.fold_in(rng, 6), dim), (blocks,), jnp.float32, low / len(cuts), high / len(cuts))
        level = level * jnp.repeat(jnp.exp(heights), dims[dim] // blocks).reshape((-1,) + (1,) * (len(dims) - 1 - dim))
    return level


def gaussian(rng, shape, scale, limit, shards=(), held_as=jnp.bfloat16):
    entries = scale * jax.random.normal(rng, shape, jnp.float32)
    if shards:
        entries = entries * levels(rng, shape, shards, -0.22, 0.18)
    return jnp.clip(entries, -limit, limit).astype(held_as)


def setup_inputs(seed: int = 0) -> dict:
    key_of = jax.random.split(jax.random.key(seed), 5)
    volume = gaussian(key_of[0], (S, Z, Y, CA, XW), 1.0, 6.0, ((1, 16),))
    weight_first = gaussian(key_of[1], (27, CB, CA), (27 * CA) ** -0.5, 0.15625, ((1, 8),))
    weight_second = gaussian(key_of[2], (27, CC, CB), (27 * CB) ** -0.5, 0.109375, ((1, 8),))
    cotangent = gaussian(key_of[3], (S, Z // 2, Y // 2, CC, XW // 2), (4.0 / (S * Z * Y * XW // 8) ** 0.5), 0.09375, ((0, 16), (3, 8)))
    return {"volume": volume, "weight_first": weight_first, "weight_second": weight_second, "cotangent": cotangent}


def pad_cells(field):
    return jnp.pad(field, ((0, 0), (1, 1), (1, 1), (0, 0), (1, 1)))

def convolve(padded, weight, depth, height, width):
    summed = None
    for offset in range(27):
        shift_depth, shift_rows, shift_cols = (offset // 9, offset // 3 % 3, offset % 3)
        window = padded[:, shift_depth:shift_depth + depth, shift_rows:shift_rows + height, :, shift_cols:shift_cols + width]
        product = jnp.einsum('oc,szycx->szyox', weight[offset].astype(jnp.float32), window.astype(jnp.float32))
        summed = product if summed is None else summed + product
    return summed

def weight_gradient(grads, padded, depth, height, width):
    parts = []
    for offset in range(27):
        shift_depth, shift_rows, shift_cols = (offset // 9, offset // 3 % 3, offset % 3)
        window = padded[:, shift_depth:shift_depth + depth, shift_rows:shift_rows + height, :, shift_cols:shift_cols + width]
        parts.append(jnp.einsum('szyox,szycx->oc', grads.astype(jnp.float32), window.astype(jnp.float32)))
    return jnp.stack(parts)

def transpose_conv(padded_grad, weight, depth, height, width):
    summed = None
    for offset in range(27):
        shift_depth, shift_rows, shift_cols = (offset // 9, offset // 3 % 3, offset % 3)
        window = padded_grad[:, 2 - shift_depth:2 - shift_depth + depth, 2 - shift_rows:2 - shift_rows + height, :, 2 - shift_cols:2 - shift_cols + width]
        product = jnp.einsum('oc,szyox->szycx', weight[offset].astype(jnp.float32), window.astype(jnp.float32))
        summed = product if summed is None else summed + product
    return summed

def reference(volume, weight_first, weight_second, cotangent):
    padded_in = pad_cells(volume)
    pre_first = convolve(padded_in, weight_first, Z, Y, XW)
    activated, pull_first = jax.vjp(jax.nn.gelu, pre_first)
    pooled = activated.reshape(S, Z // 2, 2, Y // 2, 2, CB, XW // 2, 2).mean(axis=(2, 4, 7)).astype(jnp.bfloat16)
    padded_pool = pad_cells(pooled)
    pre_second = convolve(padded_pool, weight_second, Z // 2, Y // 2, XW // 2)
    unused, pull_second = jax.vjp(jax.nn.gelu, pre_second)
    grad_out = pull_second(cotangent.astype(jnp.float32))[0].astype(jnp.bfloat16)
    grad_second = weight_gradient(grad_out, padded_pool, Z // 2, Y // 2, XW // 2)
    input_grad = transpose_conv(pad_cells(grad_out), weight_second, Z // 2, Y // 2, XW // 2)
    spread = jnp.broadcast_to(input_grad.reshape(S, Z // 2, 1, Y // 2, 1, CB, XW // 2, 1) / 8.0, (S, Z // 2, 2, Y // 2, 2, CB, XW // 2, 2))
    upsampled = spread.reshape(S, Z, Y, CB, XW)
    inner_grad = pull_first(upsampled)[0].astype(jnp.bfloat16)
    grad_first = weight_gradient(inner_grad, padded_in, Z, Y, XW)
    return (grad_first, grad_second)
```

```python
import functools

import jax
import jax.numpy as jnp
from jax import lax
from jax.experimental import pallas as pl
from jax.experimental.pallas import tpu as pltpu
from jax.sharding import PartitionSpec as P

BF = jnp.bfloat16
F32 = jnp.float32
ROOT = 0.7978845608028654
CUBE = 0.044715


def dot(a, b):
    return lax.dot_general(a, b, (((1,), (0,)), ((), ())), preferred_element_type=F32)


def dot_nt(a, b):
    return lax.dot_general(a, b, (((1,), (1,)), ((), ())), preferred_element_type=F32)


def dot_tn(a, b):
    return lax.dot_general(a, b, (((0,), (0,)), ((), ())), preferred_element_type=F32)


def gelu_and_slope(v):
    square = v * v
    t = jnp.tanh(ROOT * v * (1.0 + CUBE * square))
    half = 0.5 * (1.0 + t)
    slope = half + 0.5 * v * (1.0 - t * t) * (ROOT * (1.0 + 3.0 * CUBE * square))
    return v * half, slope


def split_shift(e):
    row = lax.broadcasted_iota(jnp.int32, (256, 256), 0)
    col = lax.broadcasted_iota(jnp.int32, (256, 256), 1)
    source = 2 * (col & 127) + (col >> 7) + (e - 1)
    return jnp.where(row == source, 1.0, 0.0).astype(BF)


def pair_shift(e):
    row = lax.broadcasted_iota(jnp.int32, (256, 256), 0)
    col = lax.broadcasted_iota(jnp.int32, (256, 256), 1)
    same = (row >> 7) == (col >> 7)
    return jnp.where(same & ((row & 127) == (col & 127) + (e - 1)), 1.0, 0.0).astype(BF)


def first_forward(own, low, high, weight, taps, slope, pooled):
    shifts = [split_shift(e) for e in range(3)]

    @pl.loop(0, 2)
    def _(s):
        for depth in range(4):
            if depth == 0:
                cells = low[s]
            elif depth == 3:
                cells = high[s]
            else:
                cells = own[s, depth - 1]
            cells = cells.reshape(256, 256)
            for e in range(3):
                taps[s, depth, :, e * 64 : (e + 1) * 64, :] = (
                    dot(cells, shifts[e]).astype(BF).reshape(4, 64, 256)
                )
        for pair in range(2):
            total = None
            for z in range(2):
                for y in (2 * pair, 2 * pair + 1):
                    first, last = max(y - 1, 0), min(y + 2, 4)
                    left = (first - y + 1) * 192
                    size = (last - first) * 192
                    pre = None
                    for a in range(3):
                        w = weight[:, a].reshape(128, 576)[:, left : left + size]
                        part = dot(w, taps[s, z + a, first:last].reshape(size, 256))
                        pre = part if pre is None else pre + part
                    value, rate = gelu_and_slope(pre)
                    slope[s, z, y] = rate
                    total = value if total is None else total + value
            pooled[s, pair] = ((total[:, :128] + total[:, 128:]) * 0.125).astype(BF)


def second_layer(parity, own, low, high, weight, cot_a, cot_b, grads, taps, mid, down, up, spread):
    left, right = pair_shift(0), pair_shift(2)
    for a, field in enumerate((low, own, high)):
        for y in range(2):
            cells = jnp.concatenate([field[0, y], field[1, y]], axis=1)
            taps[a, y, 0:128] = dot(cells, left).astype(BF)
            taps[a, y, 128:256] = cells
            taps[a, y, 256:384] = dot(cells, right).astype(BF)
    even = parity[0] == 0
    for y in range(2):
        pre = None
        for a in range(3):
            base = 9 * a + 3 * (1 - y)
            w = jnp.concatenate([weight[:, base + j].reshape(256, 128) for j in range(6)], axis=1)
            part = dot(w, taps[a].reshape(768, 256))
            pre = part if pre is None else pre + part
        _, rate = gelu_and_slope(pre)
        one = cot_a[:, y].reshape(256, 128).astype(F32)
        two = cot_b[:, y].reshape(256, 128).astype(F32)
        cot = jnp.concatenate([jnp.where(even, one, two), jnp.where(even, two, one)], axis=1)
        grad = (cot * rate).astype(BF)
        grads[y] = grad
        spread[y, 0] = dot(grad, right).astype(BF)
        spread[y, 1] = grad
        spread[y, 2] = dot(grad, left).astype(BF)
    for a, out in enumerate((down, mid, up)):
        for y in range(2):
            total = None
            for source in range(2):
                base = 9 * a + 3 * (y - source + 1)
                w = jnp.concatenate([weight[:, base + e].reshape(256, 128) for e in range(3)], axis=0)
                part = dot_tn(w, spread[source].reshape(768, 256))
                total = part if total is None else total + part
            out[y] = total.astype(out.dtype)


def second_weights(grads, taps, out):
    for a in range(3):
        for b in range(3):
            total = None
            for y in range(2):
                row = y + b - 1
                if 0 <= row < 2:
                    part = dot_nt(grads[y], taps[a, row])
                    total = part if total is None else total + part
            k = (3 * a + b) * 384
            out[:, k : k + 384] = total.astype(BF)


def first_weights(taps, slope, mid, low, high, out, total):
    total[...] = jnp.zeros_like(total)

    @pl.loop(0, 2)
    def _(s):
        for pair in range(2):
            lanes = pl.ds(pl.multiple_of(s * 128, 128), 128)
            back = (
                mid[pair, :, lanes]
                + low[pair, :, lanes].astype(F32)
                + high[pair, :, lanes].astype(F32)
            ) * 0.125
            back = jnp.concatenate([back, back], axis=1)
            for z in range(2):
                for y in (2 * pair, 2 * pair + 1):
                    inner = (slope[s, z, y] * back).astype(BF)
                    first, last = max(y - 1, 0), min(y + 2, 4)
                    left = (first - y + 1) * 192
                    size = (last - first) * 192
                    for a in range(3):
                        total[a, :, left : left + size] += dot_nt(
                            inner, taps[s, z + a, first:last].reshape(size, 256)
                        )

    out[...] = jnp.concatenate([total[a] for a in range(3)], axis=1).astype(BF)


VMEM = pl.BlockSpec(memory_space=pltpu.VMEM)
SMEM = pl.BlockSpec(memory_space=pltpu.SMEM)


def call(kernel, ins, outs, scratch, flops, name):
    shapes = [jax.ShapeDtypeStruct(s, d) for s, d in outs]
    size = sum(x.size * x.dtype.itemsize for x in list(ins) + shapes)
    return pl.pallas_call(
        kernel,
        out_shape=shapes,
        in_specs=[SMEM if x.dtype == jnp.int32 else VMEM for x in ins],
        out_specs=[VMEM] * len(outs),
        scratch_shapes=scratch,
        compiler_params=pltpu.CompilerParams(vmem_limit_bytes=48 * 1024 * 1024),
        cost_estimate=pl.CostEstimate(flops=flops, bytes_accessed=size, transcendentals=0),
        name=name,
    )(*ins)


def per_device(volume, weight_first, weight_second, cotangent):
    space, filt = lax.axis_index("space"), lax.axis_index("filt")
    ns, nf = lax.axis_size("space"), lax.axis_size("filt")
    upward = [(i, i + 1) for i in range(ns - 1)]
    downward = [(i + 1, i) for i in range(ns - 1)]

    own = lax.dynamic_slice_in_dim(volume, 2 * filt, 2, axis=0)
    low = lax.ppermute(own[:, 1], "space", upward)
    high = lax.ppermute(own[:, 0], "space", downward)

    piece = weight_first.reshape(3, 9, 16, 64).transpose(0, 2, 1, 3).reshape(3, 16, 576)
    whole_first = lax.all_to_all(
        jnp.broadcast_to(piece[None], (nf,) + piece.shape), "filt", 0, 0, tiled=True
    )
    whole_second = lax.all_gather(weight_second, "filt", axis=0, tiled=False)

    cot = lax.all_to_all(cotangent.reshape(nf, 2, 2, 32, 128), "filt", 0, 0, tiled=True)
    parity = space % 2
    same = [
        (s * nf + f, (2 * f + s % 2) * nf + s // 2) for s in range(ns) for f in range(nf)
    ]
    other = [
        (s * nf + f, (2 * f + 1 - s % 2) * nf + s // 2) for s in range(ns) for f in range(nf)
    ]
    cot_a = lax.ppermute(
        lax.dynamic_index_in_dim(cot, parity, axis=1, keepdims=False), ("space", "filt"), same
    )
    cot_b = lax.ppermute(
        lax.dynamic_index_in_dim(cot, 1 - parity, axis=1, keepdims=False), ("space", "filt"), other
    )

    taps, slope, pooled = call(
        first_forward,
        (own, low, high, whole_first),
        (((2, 4, 4, 192, 256), BF), ((2, 2, 4, 128, 256), F32), ((2, 2, 128, 128), BF)),
        [],
        2_600_000_000,
        "first_forward",
    )
    pool_low = lax.ppermute(pooled, "space", upward)
    pool_high = lax.ppermute(pooled, "space", downward)

    parity_ref = parity.astype(jnp.int32).reshape(1)
    grads, taps_second, mid, down, up = call(
        second_layer,
        (parity_ref, pooled, pool_low, pool_high, whole_second, cot_a, cot_b),
        (
            ((2, 256, 256), BF),
            ((3, 2, 384, 256), BF),
            ((2, 128, 256), F32),
            ((2, 128, 256), BF),
            ((2, 128, 256), BF),
        ),
        [pltpu.VMEM((2, 3, 256, 256), BF)],
        2_000_000_000,
        "second_layer",
    )
    from_high = lax.ppermute(down, "space", downward)
    from_low = lax.ppermute(up, "space", upward)
    (terms_second,) = call(
        second_weights,
        (grads, taps_second),
        (((256, 3456), BF),),
        [],
        900_000_000,
        "second_weights",
    )
    (terms_first,) = call(
        first_weights,
        (taps, slope, mid, from_low, from_high),
        (((128, 1728), BF),),
        [pltpu.VMEM((3, 128, 576), F32)],
        1_800_000_000,
        "first_weights",
    )

    def reduce(terms, rows):
        count = ns * nf
        got = lax.all_to_all(
            terms.reshape(count, rows, -1), ("filt", "space"), 0, 0, tiled=True
        )
        return jnp.sum(got.astype(F32), axis=0)

    mine_second = reduce(terms_second, 2)
    mine_first = reduce(terms_first, 1)
    mine = jnp.concatenate([mine_first.reshape(-1), mine_second.reshape(-1)])
    both = lax.all_to_all(
        jnp.broadcast_to(mine[None], (ns,) + mine.shape), "space", 0, 0, tiled=True
    )
    grad_first = both[:, :1728].reshape(16, 27, 64).transpose(1, 0, 2)
    grad_second = both[:, 1728:].reshape(32, 27, 128).transpose(1, 0, 2)
    return (grad_first, grad_second)


def solution(mesh):
    return jax.shard_map(
        per_device,
        mesh=mesh,
        in_specs=(
            P(None, "space", None, None, None),
            P(None, "filt", None),
            P(None, "filt", None),
            P("space", None, None, "filt", None),
        ),
        out_specs=(P(None, "filt", None), P(None, "filt", None)),
        check_vma=False,
    )
```

```python
import functools

import jax
import jax.numpy as jnp
from jax import lax
from jax.experimental import pallas as pl
from jax.experimental.pallas import tpu as pltpu
from jax.sharding import PartitionSpec as P

BF = jnp.bfloat16
F32 = jnp.float32
ROOT = 0.7978845608028654
CUBE = 0.044715


def dot(a, b):
    return lax.dot_general(a, b, (((1,), (0,)), ((), ())), preferred_element_type=F32)


def dot_nt(a, b):
    return lax.dot_general(a, b, (((1,), (1,)), ((), ())), preferred_element_type=F32)


def dot_tn(a, b):
    return lax.dot_general(a, b, (((0,), (0,)), ((), ())), preferred_element_type=F32)


def gelu_and_slope(v):
    square = v * v
    t = jnp.tanh(ROOT * v * (1.0 + CUBE * square))
    half = 0.5 * (1.0 + t)
    slope = half + 0.5 * v * (1.0 - t * t) * (ROOT * (1.0 + 3.0 * CUBE * square))
    return v * half, slope


def split_shift(e):
    row = lax.broadcasted_iota(jnp.int32, (256, 256), 0)
    col = lax.broadcasted_iota(jnp.int32, (256, 256), 1)
    source = 2 * (col & 127) + (col >> 7) + (e - 1)
    return jnp.where(row == source, 1.0, 0.0).astype(BF)


def pair_shift(e):
    row = lax.broadcasted_iota(jnp.int32, (256, 256), 0)
    col = lax.broadcasted_iota(jnp.int32, (256, 256), 1)
    same = (row >> 7) == (col >> 7)
    return jnp.where(same & ((row & 127) == (col & 127) + (e - 1)), 1.0, 0.0).astype(BF)


def pack_inputs(weight, cot, out):
    for a in range(3):
        for j in range(0, 8, 2):
            pair = jnp.concatenate([weight[9 * a + j], weight[9 * a + j + 1]], axis=1)
            for f in range(8):
                out[f, a * 64 + j * 8 : a * 64 + j * 8 + 16] = pair
    pair = jnp.concatenate([weight[8], weight[17]], axis=1)
    last = jnp.concatenate([weight[26], jnp.zeros_like(weight[26])], axis=1)
    for f in range(8):
        out[f, 192:208] = pair
        out[f, 208:224] = last
        out[f, 224:352] = cot[0, 2 * f : 2 * f + 2].reshape(128, 128)


def first_rows(packed, a):
    tiles = [packed[:, a * 64 + j * 16 : a * 64 + j * 16 + 16].reshape(128, 128) for j in range(4)]
    row = 208 if a == 2 else 192
    tiles.append(packed[:, row : row + 16].reshape(128, 128)[:, 64 * (a % 2) : 64 * (a % 2) + 64])
    return jnp.concatenate(tiles, axis=1)


def low_and_high(place, one, two):
    even = place[0] == 0
    two = jnp.where(place[2] == 1, jnp.zeros_like(two), two)
    return jnp.where(even, two, one), jnp.where(even, one, two)


def first_forward(place, own, one, two, packed, taps, slope, pooled, weight):
    shifts = [split_shift(e) for e in range(3)]
    for a in range(3):
        weight[a] = first_rows(packed, a)

    @pl.loop(0, 2)
    def _(s):
        low, high = low_and_high(place, one[s], two[s])
        for depth, cells in enumerate((low, own[s, 0], own[s, 1], high)):
            cells = cells.reshape(256, 256)
            for e in range(3):
                taps[s, depth, :, e * 64 : (e + 1) * 64, :] = (
                    dot(cells, shifts[e]).astype(BF).reshape(4, 64, 256)
                )
        for pair in range(2):
            total = None
            for z in range(2):
                for y in (2 * pair, 2 * pair + 1):
                    first, last = max(y - 1, 0), min(y + 2, 4)
                    left = (first - y + 1) * 192
                    size = (last - first) * 192
                    pre = None
                    for a in range(3):
                        w = weight[a, :, left : left + size]
                        part = dot(w, taps[s, z + a, first:last].reshape(size, 256))
                        pre = part if pre is None else pre + part
                    value, rate = gelu_and_slope(pre)
                    slope[s, z, y] = rate
                    total = value if total is None else total + value
            pooled[s, pair] = ((total[:, :128] + total[:, 128:]) * 0.125).astype(BF)


def other_blocks(place):
    filt = place[1]
    return [filt ^ (2 * d + c) for c in range(2) for d in range(4)]


def split_cot(place, packed, same, other):
    for f in range(8):
        same[f] = packed[f, pl.ds(pl.multiple_of(224 + 64 * place[0], 32), 64)]
        other[f] = packed[f, pl.ds(pl.multiple_of(288 - 64 * place[0], 32), 64)]


def join_cot(place, same, other, out):
    even = place[0] == 0
    blocks = other_blocks(place)
    for y in range(2):
        here = pl.ds(32 * y, 32)
        a = jnp.concatenate([same[f, here] for f in blocks], axis=0)
        b = jnp.concatenate([other[f, here] for f in blocks], axis=0)
        out[y, :, 0:128] = jnp.where(even, a, b)
        out[y, :, 128:256] = jnp.where(even, b, a)


def second_layer(place, own, one, two, weight, across, cot, grads, taps, mid, first, second, spread):
    even = place[0] == 0

    def rows(k):
        return jnp.concatenate([weight[:, k].reshape(128, 128), across[:, k].reshape(128, 128)], axis=0)

    left, right = pair_shift(0), pair_shift(2)
    for y in range(2):
        low, high = low_and_high(
            place,
            jnp.concatenate([one[0, y], one[1, y]], axis=1),
            jnp.concatenate([two[0, y], two[1, y]], axis=1),
        )
        mine = jnp.concatenate([own[0, y], own[1, y]], axis=1)
        for a, cells in enumerate((low, mine, high)):
            taps[a, y, 0:128] = dot(cells, left).astype(BF)
            taps[a, y, 128:256] = cells
            taps[a, y, 256:384] = dot(cells, right).astype(BF)
    for y in range(2):
        pre = None
        for a in range(3):
            base = 9 * a + 3 * (1 - y)
            w = jnp.concatenate([rows(base + j) for j in range(6)], axis=1)
            part = dot(w, taps[a].reshape(768, 256))
            pre = part if pre is None else pre + part
        _, rate = gelu_and_slope(pre)
        grad = (cot[y].astype(F32) * rate).astype(BF)
        grads[y] = grad
        spread[y, 0] = dot(grad, right).astype(BF)
        spread[y, 1] = grad
        spread[y, 2] = dot(grad, left).astype(BF)
    for y in range(2):
        parts = []
        for a in range(3):
            total = None
            for source in range(2):
                base = 9 * a + 3 * (y - source + 1)
                w = jnp.concatenate([rows(base + e) for e in range(3)], axis=0)
                part = dot_tn(w, spread[source].reshape(768, 256))
                total = part if total is None else total + part
            parts.append(total)
        down, mid[y], up = parts
        first[y] = jnp.where(even, up, down).astype(BF)
        second[y] = jnp.where(even, down, up).astype(BF)


def second_weights(grads, taps, mine, across):
    for a in range(3):
        for b in range(3):
            total = None
            for y in range(2):
                row = y + b - 1
                if 0 <= row < 2:
                    part = dot_nt(grads[y], taps[a, row])
                    total = part if total is None else total + part
            total = total.astype(BF)
            for e in range(3):
                k = 9 * a + 3 * b + e
                lanes = slice(e * 128, (e + 1) * 128)
                mine[:, k] = total[:128, lanes].reshape(4, 32, 128)
                across[:, k] = total[128:, lanes].reshape(4, 32, 128)


def add_cores(mine, across, own, *others):
    own[...] = mine[0].astype(F32) + across[0].astype(F32)
    for d, out in enumerate(others):
        out[...] = (mine[d + 1].astype(F32) + across[d + 1].astype(F32)).astype(BF)


def first_weights(place, taps, slope, mid, one, two, out, total):
    inside = place[2] == 0
    total[...] = jnp.zeros_like(total)

    @pl.loop(0, 2)
    def _(s):
        for pair in range(2):
            lanes = pl.ds(pl.multiple_of(s * 128, 128), 128)
            back = (
                mid[pair, :, lanes]
                + one[pair, :, lanes].astype(F32)
                + jnp.where(inside, two[pair, :, lanes].astype(F32), 0.0)
            ) * 0.125
            back = jnp.concatenate([back, back], axis=1)
            for z in range(2):
                for y in (2 * pair, 2 * pair + 1):
                    inner = (slope[s, z, y] * back).astype(BF)
                    first, last = max(y - 1, 0), min(y + 2, 4)
                    left = (first - y + 1) * 192
                    size = (last - first) * 192
                    for a in range(3):
                        total[a, :, left : left + size] += dot_nt(
                            inner, taps[s, z + a, first:last].reshape(size, 256)
                        )

    for a in range(3):
        out[:, a] = total[a].astype(BF).reshape(8, 16, 576)


def add_across(own, one, two, three, out):
    out[...] = (
        own[...] + one[...].astype(F32) + two[...].astype(F32) + three[...].astype(F32)
    ).astype(out.dtype)


def pack(first, second, out):
    out[0:864] = second[...].reshape(864, 128)
    for a in range(3):
        total = first[0, a].astype(F32)
        for f in range(1, 8):
            total = total + first[f, a].astype(F32)
        total = total.astype(out.dtype)
        for j in range(4):
            row = 864 + a * 64 + j * 16
            out[row : row + 16] = total[:, j * 128 : (j + 1) * 128]
        row = 1056 + a * 16
        last = total[:, 512:576]
        out[row : row + 16] = jnp.concatenate([last, jnp.zeros_like(last)], axis=1)
    out[1104:1152] = jnp.zeros((48, 128), out.dtype)


def add_up(parts, out):
    total = parts[0].astype(F32)
    for s in range(1, 16):
        total = total + parts[s].astype(F32)
    total = total.astype(out.dtype)
    for s in range(16):
        out[s] = total


def unpack(rows, first, second):
    for k in range(27):
        second[k] = rows[k * 32 : (k + 1) * 32].astype(F32)
    for a in range(3):
        for j in range(9):
            row = 864 + a * 64 + (j // 2) * 16 if j < 8 else 1056 + a * 16
            half = (j % 2) * 64
            first[9 * a + j] = rows[row : row + 16].astype(F32)[:, half : half + 64]


VMEM = pl.BlockSpec(memory_space=pltpu.VMEM)
HBM = pl.BlockSpec(memory_space=pltpu.HBM)
SMEM = pl.BlockSpec(memory_space=pltpu.SMEM)


def call(kernel, ins, outs, scratch, flops, name, far_in=(), far=(), limit=24):
    shapes = [jax.ShapeDtypeStruct(s, d) for s, d in outs]
    size = sum(x.size * x.dtype.itemsize for x in list(ins) + shapes)
    return pl.pallas_call(
        kernel,
        out_shape=shapes,
        in_specs=[
            SMEM if x.dtype == jnp.int32 else HBM if i in far_in else VMEM for i, x in enumerate(ins)
        ],
        out_specs=[HBM if i in far else VMEM for i in range(len(outs))],
        scratch_shapes=scratch,
        compiler_params=pltpu.CompilerParams(vmem_limit_bytes=limit * 1024 * 1024),
        cost_estimate=pl.CostEstimate(flops=flops, bytes_accessed=size, transcendentals=0),
        name=name,
    )(*ins)


SEND = jnp.bfloat16
LONG = 20_000_000_000


def after(value, *others):
    return lax.optimization_barrier((value,) + others)[0]


def per_device(volume, weight_first, weight_second, cotangent):
    space, filt = lax.axis_index("space"), lax.axis_index("filt")
    ns, nf = lax.axis_size("space"), lax.axis_size("filt")
    parity = space % 2
    edge = ((space == 0) | (space == ns - 1)).astype(jnp.int32)
    place = jnp.stack([parity, filt, edge])
    ones = [(i, i ^ 1) for i in range(ns)]
    twos = [(i, (((i + 1) ^ 1) - 1) % ns) for i in range(ns)]

    by_x = [[(i, i ^ (2 * d)) for i in range(nf)] for d in range(4)]
    by_core = [(i, i ^ 1) for i in range(nf)]

    def face(depth):
        zero = jnp.int32(0)
        cells = lax.dynamic_slice(volume, (2 * filt, depth, zero, zero, zero), (2, 1, 4, 64, 256))
        return cells[:, 0]

    one = lax.ppermute(face(1 - parity), "space", ones)
    two = lax.ppermute(face(parity), "space", twos)
    own = lax.dynamic_slice_in_dim(volume, 2 * filt, 2, axis=0)
    (pieces,) = call(
        pack_inputs, (weight_first, cotangent), (((8, 352, 128), BF),), [], 0, "pack_inputs", limit=60
    )
    packed = lax.all_to_all(pieces, "filt", 0, 0, tiled=True)
    weights = [weight_second] + [
        lax.ppermute(after(weight_second, pieces), "filt", by_x[d]) for d in range(1, 4)
    ]

    def turned(shift):
        return [
            (s * nf + f, (2 * f + (s + shift) % 2) * nf + s // 2)
            for s in range(ns)
            for f in range(nf)
        ]

    half = ((8, 64, 128), BF)
    cot_a, cot_b = call(split_cot, (place, packed), (half, half), [], 0, "split_cot")
    cot_a = lax.ppermute(cot_a, ("space", "filt"), turned(0))
    cot_b = lax.ppermute(cot_b, ("space", "filt"), turned(1))

    taps, slope, pooled = call(
        first_forward,
        (place, own, one, two, packed),
        (((2, 4, 4, 192, 256), BF), ((2, 2, 4, 128, 256), F32), ((2, 2, 128, 128), BF)),
        [
            pltpu.VMEM((3, 128, 576), BF),
        ],
        LONG,
        "first_forward",
    )
    pool_one = lax.ppermute(pooled, "space", ones)
    pool_two = lax.ppermute(pooled, "space", twos)
    same_core = jnp.stack([after(w, pooled) for w in weights])
    other_core = lax.ppermute(same_core, "filt", by_core)
    (cot,) = call(
        join_cot, (place, cot_a, cot_b), (((2, 256, 256), BF),), [], LONG, "join_cot"
    )
    grads, taps_second, mid, out_one, out_two = call(
        second_layer,
        (place, pooled, pool_one, pool_two, same_core, other_core, cot),
        (
            ((2, 256, 256), BF),
            ((3, 2, 384, 256), BF),
            ((2, 128, 256), F32),
            ((2, 128, 256), BF),
            ((2, 128, 256), BF),
        ),
        [pltpu.VMEM((2, 3, 256, 256), BF)],
        2_000_000_000,
        "second_layer",
    )
    back_one = lax.ppermute(out_one, "space", ones)
    back_two = lax.ppermute(out_two, "space", twos)
    mine, across = call(
        second_weights,
        (grads, taps_second),
        (((4, 27, 32, 128), BF), ((4, 27, 32, 128), BF)),
        [],
        900_000_000,
        "second_weights",
    )
    across = lax.ppermute(across, "filt", by_core)
    whole = (27, 32, 128)
    own_second, *others = call(
        add_cores, (mine, across), ((whole, F32),) + ((whole, BF),) * 3, [], 0, "add_cores"
    )
    got_second = [lax.ppermute(others[d - 1], "filt", by_x[d]) for d in range(1, 4)]
    (terms_first,) = call(
        first_weights,
        (place, taps, slope, mid, after(back_one, mine), back_two),
        (((8, 3, 16, 576), BF),),
        [pltpu.VMEM((3, 128, 576), F32)],
        LONG,
        "first_weights",
    )
    got_first = lax.all_to_all(terms_first, "filt", 0, 0, tiled=True)

    (mine_second,) = call(
        add_across, (own_second, *got_second), ((whole, SEND),), [], LONG, "add_across"
    )
    (rows,) = call(pack, (got_first, mine_second), (((1152, 128), SEND),), [], 0, "pack")
    parts = lax.all_to_all(rows.reshape(ns, 72, 128), "space", 0, 0, tiled=True)
    (mine,) = call(add_up, (parts,), (((16, 72, 128), SEND),), [], 0, "add_up")
    rows = lax.all_to_all(mine, "space", 0, 0, tiled=True).reshape(1152, 128)
    return call(
        unpack,
        (rows,),
        (((27, 16, 64), F32), ((27, 32, 128), F32)),
        [],
        0,
        "unpack",
    )


def solution(mesh):
    return jax.shard_map(
        per_device,
        mesh=mesh,
        in_specs=(
            P(None, "space", None, None, None),
            P(None, "filt", None),
            P(None, "filt", None),
            P("space", None, None, "filt", None),
        ),
        out_specs=(P(None, "filt", None), P(None, "filt", None)),
        check_vma=False,
    )
```

```python
import functools

import jax
import jax.numpy as jnp
from jax import lax
from jax.experimental import pallas as pl
from jax.experimental.pallas import tpu as pltpu
from jax.sharding import PartitionSpec as P

BF = jnp.bfloat16
F32 = jnp.float32
ROOT = 0.7978845608028654
CUBE = 0.044715


def dot(a, b):
    return lax.dot_general(a, b, (((1,), (0,)), ((), ())), preferred_element_type=F32)


def dot_nt(a, b):
    return lax.dot_general(a, b, (((1,), (1,)), ((), ())), preferred_element_type=F32)


def dot_tn(a, b):
    return lax.dot_general(a, b, (((0,), (0,)), ((), ())), preferred_element_type=F32)


def gelu_and_slope(v):
    square = v * v
    t = jnp.tanh(ROOT * v * (1.0 + CUBE * square))
    half = 0.5 * (1.0 + t)
    slope = half + 0.5 * v * (1.0 - t * t) * (ROOT * (1.0 + 3.0 * CUBE * square))
    return v * half, slope


def split_shift(e):
    row = lax.broadcasted_iota(jnp.int32, (256, 256), 0)
    col = lax.broadcasted_iota(jnp.int32, (256, 256), 1)
    source = 2 * (col & 127) + (col >> 7) + (e - 1)
    return jnp.where(row == source, 1.0, 0.0).astype(BF)


def pair_shift(e):
    row = lax.broadcasted_iota(jnp.int32, (256, 256), 0)
    col = lax.broadcasted_iota(jnp.int32, (256, 256), 1)
    same = (row >> 7) == (col >> 7)
    return jnp.where(same & ((row & 127) == (col & 127) + (e - 1)), 1.0, 0.0).astype(BF)


def pack_weights(weight, second, out):
    for a in range(3):
        for j in range(0, 8, 2):
            pair = jnp.concatenate([weight[9 * a + j], weight[9 * a + j + 1]], axis=1)
            out[a * 64 + j * 8 : a * 64 + j * 8 + 16] = pair
    out[192:208] = jnp.concatenate([weight[8], weight[17]], axis=1)
    out[208:224] = jnp.concatenate([weight[26], jnp.zeros_like(weight[26])], axis=1)
    out[224:1088] = second[...].reshape(864, 128)


def first_rows(pieces, a):
    def stacked(row):
        return jnp.concatenate([piece[row : row + 16] for piece in pieces], axis=0)

    tiles = [stacked(a * 64 + j * 16) for j in range(4)]
    tiles.append(stacked(208 if a == 2 else 192)[:, 64 * (a % 2) : 64 * (a % 2) + 64])
    return jnp.concatenate(tiles, axis=1)


def low_and_high(place, one, two):
    even = place[0] == 0
    two = jnp.where(place[2] == 1, jnp.zeros_like(two), two)
    return jnp.where(even, two, one), jnp.where(even, one, two)


def first_forward(place, own, one, two, packed, across, taps, slope, pooled, weight, edges):
    shifts = [split_shift(e) for e in range(3)]
    pieces = []
    for f in range(8):
        where = place[1] ^ f
        pieces.append(jnp.where((where & 1) == 0, packed[where >> 1], across[where >> 1]))
    parts = [first_rows(pieces, a) for a in range(3)]
    weight[...] = jnp.concatenate(parts, axis=1)
    edges[0] = jnp.concatenate([w[:, 192:] for w in parts], axis=1)
    edges[1] = jnp.concatenate([w[:, :384] for w in parts], axis=1)

    @pl.loop(0, 2)
    def _(s):
        low, high = low_and_high(place, one[s], two[s])
        for depth, cells in enumerate((low, own[s, 0], own[s, 1], high)):
            cells = cells.reshape(256, 256)
            for e in range(3):
                taps[s, depth, :, e * 64 : (e + 1) * 64, :] = (
                    dot(cells, shifts[e]).astype(BF).reshape(4, 64, 256)
                )
        for pair in range(2):
            total = None
            for z in range(2):
                for y in (2 * pair, 2 * pair + 1):
                    first, last = max(y - 1, 0), min(y + 2, 4)
                    size = (last - first) * 192
                    w = weight[...] if size == 576 else edges[y // 3]
                    cells = [taps[s, z + a, first:last].reshape(size, 256) for a in range(3)]
                    pre = dot(w, jnp.concatenate(cells, axis=0))
                    value, rate = gelu_and_slope(pre)
                    slope[s, z, y] = rate
                    total = value if total is None else total + value
            pooled[s, pair] = ((total[:, :128] + total[:, 128:]) * 0.125).astype(BF)


def other_blocks(place):
    filt = place[1]
    return [filt ^ (2 * d + c) for c in range(2) for d in range(4)]


def second_layer(place, own, one, two, weight, across, cot, grads, taps, mid, first, second, spread):
    even = place[0] == 0
    blocks = other_blocks(place)

    def rows(k):
        here = slice(224 + 32 * k, 256 + 32 * k)
        return jnp.concatenate(
            [weight[:, here].reshape(128, 128), across[:, here].reshape(128, 128)], axis=0
        )

    left, right = pair_shift(0), pair_shift(2)
    for y in range(2):
        low, high = low_and_high(
            place,
            jnp.concatenate([one[0, y], one[1, y]], axis=1),
            jnp.concatenate([two[0, y], two[1, y]], axis=1),
        )
        mine = jnp.concatenate([own[0, y], own[1, y]], axis=1)
        for a, cells in enumerate((low, mine, high)):
            taps[a, y, 0:128] = dot(cells, left).astype(BF)
            taps[a, y, 128:256] = cells
            taps[a, y, 256:384] = dot(cells, right).astype(BF)
    for y in range(2):
        pre = None
        for a in range(3):
            base = 9 * a + 3 * (1 - y)
            w = jnp.concatenate([rows(base + j) for j in range(6)], axis=1)
            part = dot(w, taps[a].reshape(768, 256))
            pre = part if pre is None else pre + part
        _, rate = gelu_and_slope(pre)
        pair = [jnp.concatenate([cot[f, j, y] for f in blocks], axis=0) for j in range(2)]
        grad = (jnp.concatenate(pair, axis=1).astype(F32) * rate).astype(BF)
        grads[y] = grad
        spread[y, 0] = dot(grad, right).astype(BF)
        spread[y, 1] = grad
        spread[y, 2] = dot(grad, left).astype(BF)
    for y in range(2):
        parts = []
        for a in range(3):
            total = None
            for source in range(2):
                base = 9 * a + 3 * (y - source + 1)
                w = jnp.concatenate([rows(base + e) for e in range(3)], axis=0)
                part = dot_tn(w, spread[source].reshape(768, 256))
                total = part if total is None else total + part
            parts.append(total)
        down, mid[y], up = parts
        first[y] = jnp.where(even, up, down).astype(BF)
        second[y] = jnp.where(even, down, up).astype(BF)


def second_weights(grads, taps, mine, across):
    for a in range(3):
        for b in range(3):
            total = None
            for y in range(2):
                row = y + b - 1
                if 0 <= row < 2:
                    part = dot_nt(grads[y], taps[a, row])
                    total = part if total is None else total + part
            total = total.astype(BF)
            for e in range(3):
                k = 9 * a + 3 * b + e
                lanes = slice(e * 128, (e + 1) * 128)
                mine[:, k] = total[:128, lanes].reshape(4, 32, 128)
                across[:, k] = total[128:, lanes].reshape(4, 32, 128)


def add_cores(mine, across, own, *others):
    own[...] = mine[0].astype(F32) + across[0].astype(F32)
    for d, out in enumerate(others):
        out[...] = (mine[d + 1].astype(F32) + across[d + 1].astype(F32)).astype(BF)


def first_weights(place, taps, slope, mid, one, two, out, total):
    inside = place[2] == 0
    total[...] = jnp.zeros_like(total)

    @pl.loop(0, 2)
    def _(s):
        for pair in range(2):
            lanes = pl.ds(pl.multiple_of(s * 128, 128), 128)
            back = (
                mid[pair, :, lanes]
                + one[pair, :, lanes].astype(F32)
                + jnp.where(inside, two[pair, :, lanes].astype(F32), 0.0)
            ) * 0.125
            back = jnp.concatenate([back, back], axis=1)
            inner = [
                jnp.concatenate(
                    [(slope[s, z, 2 * pair + i] * back).astype(BF) for i in range(2)], axis=0
                )
                for z in range(2)
            ]
            inner = jnp.concatenate(inner, axis=1)
            for a in range(3):
                cells = [
                    taps[s, z + a, pair : pair + 3].reshape(576, 256) for z in range(2)
                ]
                part = dot_nt(jnp.concatenate(cells, axis=1), inner)
                if pair == 0:
                    total[a] += part[:, 128:]
                    total[a, 192:576] += part[0:384, :128]
                else:
                    total[a] += part[:, :128]
                    total[a, 0:384] += part[192:576, 128:]

    for a in range(3):
        out[:, a] = total[a].T.astype(BF).reshape(8, 16, 576)


def add_across(own, one, two, three, out):
    out[...] = (
        own[...] + one[...].astype(F32) + two[...].astype(F32) + three[...].astype(F32)
    ).astype(out.dtype)


def pack(first, second, out):
    out[0:864] = second[...].reshape(864, 128)
    for a in range(3):
        total = first[0, a].astype(F32)
        for f in range(1, 8):
            total = total + first[f, a].astype(F32)
        total = total.astype(out.dtype)
        for j in range(4):
            row = 864 + a * 64 + j * 16
            out[row : row + 16] = total[:, j * 128 : (j + 1) * 128]
        row = 1056 + a * 16
        last = total[:, 512:576]
        out[row : row + 16] = jnp.concatenate([last, jnp.zeros_like(last)], axis=1)
    out[1104:1152] = jnp.zeros((48, 128), out.dtype)


def add_up(parts, out):
    total = parts[0].astype(F32)
    for s in range(1, 16):
        total = total + parts[s].astype(F32)
    total = total.astype(out.dtype)
    for s in range(16):
        out[s] = total


def unpack(rows, first, second):
    for k in range(27):
        second[k] = rows[k * 32 : (k + 1) * 32].astype(F32)
    for a in range(3):
        for j in range(9):
            row = 864 + a * 64 + (j // 2) * 16 if j < 8 else 1056 + a * 16
            half = (j % 2) * 64
            first[9 * a + j] = rows[row : row + 16].astype(F32)[:, half : half + 64]


VMEM = pl.BlockSpec(memory_space=pltpu.VMEM)
HBM = pl.BlockSpec(memory_space=pl.ANY)
SMEM = pl.BlockSpec(memory_space=pltpu.SMEM)


def call(kernel, ins, outs, scratch, flops, name, far_in=(), far=(), limit=24):
    shapes = [jax.ShapeDtypeStruct(s, d) for s, d in outs]
    size = sum(x.size * x.dtype.itemsize for x in list(ins) + shapes)
    return pl.pallas_call(
        kernel,
        out_shape=shapes,
        in_specs=[
            SMEM if x.dtype == jnp.int32 else HBM if i in far_in else VMEM for i, x in enumerate(ins)
        ],
        out_specs=[HBM if i in far else VMEM for i in range(len(outs))],
        scratch_shapes=scratch,
        compiler_params=pltpu.CompilerParams(vmem_limit_bytes=limit * 1024 * 1024),
        cost_estimate=pl.CostEstimate(flops=flops, bytes_accessed=size, transcendentals=0),
        name=name,
    )(*ins)


SEND = jnp.bfloat16
LONG = 20_000_000_000


def after(value, *others):
    return lax.optimization_barrier((value,) + others)[0]


def per_device(volume, weight_first, weight_second, cotangent):
    space, filt = lax.axis_index("space"), lax.axis_index("filt")
    ns, nf = lax.axis_size("space"), lax.axis_size("filt")
    parity = space % 2
    edge = ((space == 0) | (space == ns - 1)).astype(jnp.int32)
    place = jnp.stack([parity, filt, edge])
    ones = [(i, i ^ 1) for i in range(ns)]
    twos = [(i, (((i + 1) ^ 1) - 1) % ns) for i in range(ns)]

    by_x = [[(i, i ^ (2 * d)) for i in range(nf)] for d in range(4)]
    by_core = [(i, i ^ 1) for i in range(nf)]

    def face(depth):
        zero = jnp.int32(0)
        cells = lax.dynamic_slice(volume, (2 * filt, depth, zero, zero, zero), (2, 1, 4, 64, 256))
        return cells[:, 0]

    one = lax.ppermute(face(1 - parity), "space", ones)
    two = lax.ppermute(face(parity), "space", twos)
    own = lax.dynamic_slice_in_dim(volume, 2 * filt, 2, axis=0)
    by_sample = lax.all_to_all(cotangent[0], "space", 0, 0, tiled=True)
    (piece,) = call(
        pack_weights, (after(weight_first, one), weight_second), (((1088, 128), BF),), [], 0, "pack_weights"
    )
    others = [lax.ppermute(piece, "filt", by_x[d]) for d in range(1, 4)]
    cot = lax.all_to_all(by_sample.reshape(nf, 2, 2, 32, 128), "filt", 0, 0, tiled=True)
    weights = jnp.stack([after(w, own, two, cot) for w in [piece] + others])
    across = lax.ppermute(weights, "filt", by_core)

    taps, slope, pooled = call(
        first_forward,
        (place, after(own, cot), one, two, weights, across),
        (((2, 4, 4, 192, 256), BF), ((2, 2, 4, 128, 256), F32), ((2, 2, 128, 128), BF)),
        [
            pltpu.VMEM((128, 1728), BF),
            pltpu.VMEM((2, 128, 1152), BF),
        ],
        LONG,
        "first_forward",
    )
    pool_one = lax.ppermute(pooled, "space", ones)
    pool_two = lax.ppermute(pooled, "space", twos)
    grads, taps_second, mid, out_one, out_two = call(
        second_layer,
        (place, pooled, pool_one, pool_two, weights, across, cot),
        (
            ((2, 256, 256), BF),
            ((3, 2, 384, 256), BF),
            ((2, 128, 256), F32),
            ((2, 128, 256), BF),
            ((2, 128, 256), BF),
        ),
        [pltpu.VMEM((2, 3, 256, 256), BF)],
        2_000_000_000,
        "second_layer",
    )
    back_one = lax.ppermute(out_one, "space", ones)
    back_two = lax.ppermute(out_two, "space", twos)
    mine, across = call(
        second_weights,
        (grads, taps_second),
        (((4, 27, 32, 128), BF), ((4, 27, 32, 128), BF)),
        [],
        900_000_000,
        "second_weights",
    )
    across = lax.ppermute(across, "filt", by_core)
    whole = (27, 32, 128)
    own_second, *others = call(
        add_cores, (mine, across), ((whole, F32),) + ((whole, BF),) * 3, [], 0, "add_cores"
    )
    got_second = [lax.ppermute(others[d - 1], "filt", by_x[d]) for d in range(1, 4)]
    (terms_first,) = call(
        first_weights,
        (place, taps, slope, mid, after(back_one, mine), back_two),
        (((8, 3, 16, 576), BF),),
        [pltpu.VMEM((3, 576, 128), F32)],
        LONG,
        "first_weights",
    )
    got_first = lax.all_to_all(terms_first, "filt", 0, 0, tiled=True)

    (mine_second,) = call(
        add_across, (own_second, *got_second), ((whole, SEND),), [], LONG, "add_across"
    )
    (rows,) = call(pack, (got_first, mine_second), (((1152, 128), SEND),), [], 0, "pack")
    parts = lax.all_to_all(rows.reshape(ns, 72, 128), "space", 0, 0, tiled=True)
    (mine,) = call(add_up, (parts,), (((16, 72, 128), SEND),), [], 0, "add_up")
    rows = lax.all_to_all(mine, "space", 0, 0, tiled=True).reshape(1152, 128)
    return call(
        unpack,
        (rows,),
        (((27, 16, 64), F32), ((27, 32, 128), F32)),
        [],
        0,
        "unpack",
    )


def solution(mesh):
    return jax.shard_map(
        per_device,
        mesh=mesh,
        in_specs=(
            P(None, "space", None, None, None),
            P(None, "filt", None),
            P(None, "filt", None),
            P("space", None, None, "filt", None),
        ),
        out_specs=(P(None, "filt", None), P(None, "filt", None)),
        check_vma=False,
    )
```

```python
import functools

import jax
import jax.numpy as jnp
from jax import lax
from jax.experimental import pallas as pl
from jax.experimental.pallas import tpu as pltpu
from jax.sharding import PartitionSpec as P

BF = jnp.bfloat16
F32 = jnp.float32
ROOT = 0.7978845608028654
CUBE = 0.044715


def dot(a, b):
    return lax.dot_general(a, b, (((1,), (0,)), ((), ())), preferred_element_type=F32)


def dot_nt(a, b):
    return lax.dot_general(a, b, (((1,), (1,)), ((), ())), preferred_element_type=F32)


def dot_tn(a, b):
    return lax.dot_general(a, b, (((0,), (0,)), ((), ())), preferred_element_type=F32)


def gelu_and_slope(v):
    square = v * v
    t = jnp.tanh(ROOT * v * (1.0 + CUBE * square))
    half = 0.5 * (1.0 + t)
    slope = half + 0.5 * v * (1.0 - t * t) * (ROOT * (1.0 + 3.0 * CUBE * square))
    return v * half, slope


def split_shift(e):
    row = lax.broadcasted_iota(jnp.int32, (256, 256), 0)
    col = lax.broadcasted_iota(jnp.int32, (256, 256), 1)
    source = 2 * (col & 127) + (col >> 7) + (e - 1)
    return jnp.where(row == source, 1.0, 0.0).astype(BF)


def pair_shift(e):
    row = lax.broadcasted_iota(jnp.int32, (256, 256), 0)
    col = lax.broadcasted_iota(jnp.int32, (256, 256), 1)
    same = (row >> 7) == (col >> 7)
    return jnp.where(same & ((row & 127) == (col & 127) + (e - 1)), 1.0, 0.0).astype(BF)


def pack_weights(weight, second, out):
    for a in range(3):
        for j in range(0, 8, 2):
            pair = jnp.concatenate([weight[9 * a + j], weight[9 * a + j + 1]], axis=1)
            out[a * 64 + j * 8 : a * 64 + j * 8 + 16] = pair
    out[192:208] = jnp.concatenate([weight[8], weight[17]], axis=1)
    out[208:224] = jnp.concatenate([weight[26], jnp.zeros_like(weight[26])], axis=1)
    out[224:1088] = second[...].reshape(864, 128)


def first_rows(pieces, a):
    def stacked(row):
        return jnp.concatenate([piece[row : row + 16] for piece in pieces], axis=0)

    tiles = [stacked(a * 64 + j * 16) for j in range(4)]
    tiles.append(stacked(208 if a == 2 else 192)[:, 64 * (a % 2) : 64 * (a % 2) + 64])
    return jnp.concatenate(tiles, axis=1)


def deal_cot(place, cot, *outs):
    for d, out in enumerate(outs):
        here = (place[1] >> 1) ^ d
        for j in range(4):
            out[j] = cot[4 * here + j]


def sort_cot(place, p0, p1, p2, p3, mine, across):
    core = place[1] & 1
    for d, piece in enumerate((p0, p1, p2, p3)):
        for j in range(2):
            mine[d, j] = piece[2 * core + j]
            across[d, j] = piece[2 - 2 * core + j]


def low_and_high(place, one, two):
    even = place[0] == 0
    two = jnp.where(place[2] == 1, jnp.zeros_like(two), two)
    return jnp.where(even, two, one), jnp.where(even, one, two)


def first_forward(place, own, one, two, packed, across, taps, slope, pooled, weight, edges):
    shifts = [split_shift(e) for e in range(3)]
    pieces = []
    for f in range(8):
        where = place[1] ^ f
        pieces.append(jnp.where((where & 1) == 0, packed[where >> 1], across[where >> 1]))
    parts = [first_rows(pieces, a) for a in range(3)]
    weight[...] = jnp.concatenate(parts, axis=1)
    edges[0] = jnp.concatenate([w[:, 192:] for w in parts], axis=1)
    edges[1] = jnp.concatenate([w[:, :384] for w in parts], axis=1)

    @pl.loop(0, 2)
    def _(s):
        low, high = low_and_high(place, one[s], two[s])
        for depth, cells in enumerate((low, own[s, 0], own[s, 1], high)):
            cells = cells.reshape(256, 256)
            for e in range(3):
                taps[s, depth, :, e * 64 : (e + 1) * 64, :] = (
                    dot(cells, shifts[e]).astype(BF).reshape(4, 64, 256)
                )
        for pair in range(2):
            total = None
            for z in range(2):
                for y in (2 * pair, 2 * pair + 1):
                    first, last = max(y - 1, 0), min(y + 2, 4)
                    size = (last - first) * 192
                    w = weight[...] if size == 576 else edges[y // 3]
                    cells = [taps[s, z + a, first:last].reshape(size, 256) for a in range(3)]
                    pre = dot(w, jnp.concatenate(cells, axis=0))
                    value, rate = gelu_and_slope(pre)
                    slope[s, z, y] = rate
                    total = value if total is None else total + value
            pooled[s, pair] = ((total[:, :128] + total[:, 128:]) * 0.125).astype(BF)


def second_layer(
    place, own, one, two, weight, across, cot, cot_across, grads, taps, mid, first, second, spread
):
    even = place[0] == 0

    def rows(k):
        here = slice(224 + 32 * k, 256 + 32 * k)
        return jnp.concatenate(
            [weight[:, here].reshape(128, 128), across[:, here].reshape(128, 128)], axis=0
        )

    left, right = pair_shift(0), pair_shift(2)
    for y in range(2):
        low, high = low_and_high(
            place,
            jnp.concatenate([one[0, y], one[1, y]], axis=1),
            jnp.concatenate([two[0, y], two[1, y]], axis=1),
        )
        mine = jnp.concatenate([own[0, y], own[1, y]], axis=1)
        for a, cells in enumerate((low, mine, high)):
            taps[a, y, 0:128] = dot(cells, left).astype(BF)
            taps[a, y, 128:256] = cells
            taps[a, y, 256:384] = dot(cells, right).astype(BF)
    for y in range(2):
        pre = None
        for a in range(3):
            base = 9 * a + 3 * (1 - y)
            w = jnp.concatenate([rows(base + j) for j in range(6)], axis=1)
            part = dot(w, taps[a].reshape(768, 256))
            pre = part if pre is None else pre + part
        _, rate = gelu_and_slope(pre)
        pair = [
            jnp.concatenate([c[d, j, y] for c in (cot, cot_across) for d in range(4)], axis=0)
            for j in range(2)
        ]
        grad = (jnp.concatenate(pair, axis=1).astype(F32) * rate).astype(BF)
        grads[y] = grad
        spread[y, 0] = dot(grad, right).astype(BF)
        spread[y, 1] = grad
        spread[y, 2] = dot(grad, left).astype(BF)
    for y in range(2):
        parts = []
        for a in range(3):
            total = None
            for source in range(2):
                base = 9 * a + 3 * (y - source + 1)
                w = jnp.concatenate([rows(base + e) for e in range(3)], axis=0)
                part = dot_tn(w, spread[source].reshape(768, 256))
                total = part if total is None else total + part
            parts.append(total)
        down, mid[y], up = parts
        first[y] = jnp.where(even, up, down).astype(BF)
        second[y] = jnp.where(even, down, up).astype(BF)


def second_weights(grads, taps, mine, across):
    for a in range(3):
        for b in range(3):
            total = None
            for y in range(2):
                row = y + b - 1
                if 0 <= row < 2:
                    part = dot_nt(grads[y], taps[a, row])
                    total = part if total is None else total + part
            total = total.astype(BF)
            for e in range(3):
                k = 9 * a + 3 * b + e
                lanes = slice(e * 128, (e + 1) * 128)
                mine[:, k] = total[:128, lanes].reshape(4, 32, 128)
                across[:, k] = total[128:, lanes].reshape(4, 32, 128)


def add_cores(mine, across, own, *others):
    own[...] = mine[0].astype(F32) + across[0].astype(F32)
    for d, out in enumerate(others):
        out[...] = (mine[d + 1].astype(F32) + across[d + 1].astype(F32)).astype(BF)


def first_weights(place, taps, slope, mid, one, two, out, total):
    inside = place[2] == 0
    total[...] = jnp.zeros_like(total)

    @pl.loop(0, 2)
    def _(s):
        for pair in range(2):
            lanes = pl.ds(pl.multiple_of(s * 128, 128), 128)
            back = (
                mid[pair, :, lanes]
                + one[pair, :, lanes].astype(F32)
                + jnp.where(inside, two[pair, :, lanes].astype(F32), 0.0)
            ) * 0.125
            back = jnp.concatenate([back, back], axis=1)
            inner = [
                jnp.concatenate(
                    [(slope[s, z, 2 * pair + i] * back).astype(BF) for i in range(2)], axis=0
                )
                for z in range(2)
            ]
            inner = jnp.concatenate(inner, axis=1)
            for a in range(3):
                cells = [
                    taps[s, z + a, pair : pair + 3].reshape(576, 256) for z in range(2)
                ]
                part = dot_nt(jnp.concatenate(cells, axis=1), inner)
                if pair == 0:
                    total[a] += part[:, 128:]
                    total[a, 192:576] += part[0:384, :128]
                else:
                    total[a] += part[:, :128]
                    total[a, 0:384] += part[192:576, 128:]

    for a in range(3):
        out[:, a] = total[a].T.astype(BF).reshape(8, 16, 576)


def add_across(own, one, two, three, out):
    out[...] = (
        own[...] + one[...].astype(F32) + two[...].astype(F32) + three[...].astype(F32)
    ).astype(out.dtype)


def pack(first, second, out):
    out[0:864] = second[...].reshape(864, 128)
    for a in range(3):
        total = first[0, a].astype(F32)
        for f in range(1, 8):
            total = total + first[f, a].astype(F32)
        total = total.astype(out.dtype)
        for j in range(4):
            row = 864 + a * 64 + j * 16
            out[row : row + 16] = total[:, j * 128 : (j + 1) * 128]
        row = 1056 + a * 16
        last = total[:, 512:576]
        out[row : row + 16] = jnp.concatenate([last, jnp.zeros_like(last)], axis=1)
    out[1104:1152] = jnp.zeros((48, 128), out.dtype)


def add_up(parts, out):
    total = parts[0].astype(F32)
    for s in range(1, 16):
        total = total + parts[s].astype(F32)
    total = total.astype(out.dtype)
    for s in range(16):
        out[s] = total


def unpack(rows, first, second):
    for k in range(27):
        second[k] = rows[k * 32 : (k + 1) * 32].astype(F32)
    for a in range(3):
        for j in range(9):
            row = 864 + a * 64 + (j // 2) * 16 if j < 8 else 1056 + a * 16
            half = (j % 2) * 64
            first[9 * a + j] = rows[row : row + 16].astype(F32)[:, half : half + 64]


VMEM = pl.BlockSpec(memory_space=pltpu.VMEM)
HBM = pl.BlockSpec(memory_space=pl.ANY)
SMEM = pl.BlockSpec(memory_space=pltpu.SMEM)


def call(kernel, ins, outs, scratch, flops, name, far_in=(), far=(), limit=24):
    shapes = [jax.ShapeDtypeStruct(s, d) for s, d in outs]
    size = sum(x.size * x.dtype.itemsize for x in list(ins) + shapes)
    return pl.pallas_call(
        kernel,
        out_shape=shapes,
        in_specs=[
            SMEM if x.dtype == jnp.int32 else HBM if i in far_in else VMEM for i, x in enumerate(ins)
        ],
        out_specs=[HBM if i in far else VMEM for i in range(len(outs))],
        scratch_shapes=scratch,
        compiler_params=pltpu.CompilerParams(vmem_limit_bytes=limit * 1024 * 1024),
        cost_estimate=pl.CostEstimate(flops=flops, bytes_accessed=size, transcendentals=0),
        name=name,
    )(*ins)


SEND = jnp.bfloat16
LONG = 20_000_000_000


def after(value, *others):
    return lax.optimization_barrier((value,) + others)[0]


def per_device(volume, weight_first, weight_second, cotangent):
    space, filt = lax.axis_index("space"), lax.axis_index("filt")
    ns, nf = lax.axis_size("space"), lax.axis_size("filt")
    parity = space % 2
    edge = ((space == 0) | (space == ns - 1)).astype(jnp.int32)
    place = jnp.stack([parity, filt, edge])
    ones = [(i, i ^ 1) for i in range(ns)]
    twos = [(i, (((i + 1) ^ 1) - 1) % ns) for i in range(ns)]

    by_x = [[(i, i ^ (2 * d)) for i in range(nf)] for d in range(4)]
    by_core = [(i, i ^ 1) for i in range(nf)]

    def face(depth):
        zero = jnp.int32(0)
        cells = lax.dynamic_slice(volume, (2 * filt, depth, zero, zero, zero), (2, 1, 4, 64, 256))
        return cells[:, 0]

    outer, inner = face(1 - parity), face(parity)
    one = lax.ppermute(outer, "space", ones)
    two = lax.ppermute(inner, "space", twos)
    by_sample = lax.all_to_all(cotangent[0], "space", 0, 0, tiled=True)
    (piece,) = call(
        pack_weights, (after(weight_first, outer, inner), weight_second), (((1088, 128), BF),), [], 0, "pack_weights"
    )
    others = [lax.ppermute(piece, "filt", by_x[d]) for d in range(1, 4)]
    own = lax.dynamic_slice_in_dim(after(volume, by_sample), 2 * filt, 2, axis=0)
    weights = jnp.stack([after(w, by_sample, one, two) for w in [piece] + others])
    across = lax.ppermute(weights, "filt", by_core)

    part = ((4, 2, 32, 128), BF)
    pieces = call(deal_cot, (place, by_sample), (part,) * 4, [], 0, "deal_cot")
    pieces = [pieces[0]] + [lax.ppermute(pieces[d], "filt", by_x[d]) for d in range(1, 4)]

    taps, slope, pooled = call(
        first_forward,
        (place, own, one, two, weights, across),
        (((2, 4, 4, 192, 256), BF), ((2, 2, 4, 128, 256), F32), ((2, 2, 128, 128), BF)),
        [
            pltpu.VMEM((128, 1728), BF),
            pltpu.VMEM((2, 128, 1152), BF),
        ],
        LONG,
        "first_forward",
    )
    pool_one = lax.ppermute(pooled, "space", ones)
    pool_two = lax.ppermute(pooled, "space", twos)
    half = ((4, 2, 2, 32, 128), BF)
    cot, cot_across = call(sort_cot, (place, after(pieces[0], pooled), *pieces[1:]), (half, half), [], 0, "sort_cot")
    cot_across = lax.ppermute(cot_across, "filt", by_core)
    grads, taps_second, mid, out_one, out_two = call(
        second_layer,
        (place, pooled, pool_one, pool_two, weights, across, cot, cot_across),
        (
            ((2, 256, 256), BF),
            ((3, 2, 384, 256), BF),
            ((2, 128, 256), F32),
            ((2, 128, 256), BF),
            ((2, 128, 256), BF),
        ),
        [pltpu.VMEM((2, 3, 256, 256), BF)],
        2_000_000_000,
        "second_layer",
    )
    back_one = lax.ppermute(out_one, "space", ones)
    back_two = lax.ppermute(out_two, "space", twos)
    mine, across = call(
        second_weights,
        (grads, taps_second),
        (((4, 27, 32, 128), BF), ((4, 27, 32, 128), BF)),
        [],
        900_000_000,
        "second_weights",
    )
    across = lax.ppermute(across, "filt", by_core)
    whole = (27, 32, 128)
    own_second, *others = call(
        add_cores, (mine, across), ((whole, F32),) + ((whole, BF),) * 3, [], 0, "add_cores"
    )
    got_second = [lax.ppermute(others[d - 1], "filt", by_x[d]) for d in range(1, 4)]
    (terms_first,) = call(
        first_weights,
        (place, taps, slope, mid, after(back_one, mine), back_two),
        (((8, 3, 16, 576), BF),),
        [pltpu.VMEM((3, 576, 128), F32)],
        LONG,
        "first_weights",
    )
    got_first = lax.all_to_all(terms_first, "filt", 0, 0, tiled=True)

    (mine_second,) = call(
        add_across, (own_second, *got_second), ((whole, SEND),), [], LONG, "add_across"
    )
    (rows,) = call(pack, (got_first, mine_second), (((1152, 128), SEND),), [], 0, "pack")
    parts = lax.all_to_all(rows.reshape(ns, 72, 128), "space", 0, 0, tiled=True)
    (mine,) = call(add_up, (parts,), (((16, 72, 128), SEND),), [], 0, "add_up")
    rows = lax.all_to_all(mine, "space", 0, 0, tiled=True).reshape(1152, 128)
    return call(
        unpack,
        (rows,),
        (((27, 16, 64), F32), ((27, 32, 128), F32)),
        [],
        0,
        "unpack",
    )


def solution(mesh):
    return jax.shard_map(
        per_device,
        mesh=mesh,
        in_specs=(
            P(None, "space", None, None, None),
            P(None, "filt", None),
            P(None, "filt", None),
            P("space", None, None, "filt", None),
        ),
        out_specs=(P(None, "filt", None), P(None, "filt", None)),
        check_vma=False,
    )
```

```python
import functools

import jax
import jax.numpy as jnp
from jax import lax
from jax.experimental import pallas as pl
from jax.experimental.pallas import tpu as pltpu
from jax.sharding import PartitionSpec as P

BF = jnp.bfloat16
F32 = jnp.float32
ROOT = 0.7978845608028654
CUBE = 0.044715


def dot(a, b):
    return lax.dot_general(a, b, (((1,), (0,)), ((), ())), preferred_element_type=F32)


def dot_nt(a, b):
    return lax.dot_general(a, b, (((1,), (1,)), ((), ())), preferred_element_type=F32)


def dot_tn(a, b):
    return lax.dot_general(a, b, (((0,), (0,)), ((), ())), preferred_element_type=F32)


def gelu_and_slope(v):
    square = v * v
    t = jnp.tanh(ROOT * v * (1.0 + CUBE * square))
    half = 0.5 * (1.0 + t)
    slope = half + 0.5 * v * (1.0 - t * t) * (ROOT * (1.0 + 3.0 * CUBE * square))
    return v * half, slope


def split_shift(e):
    row = lax.broadcasted_iota(jnp.int32, (256, 256), 0)
    col = lax.broadcasted_iota(jnp.int32, (256, 256), 1)
    source = 2 * (col & 127) + (col >> 7) + (e - 1)
    return jnp.where(row == source, 1.0, 0.0).astype(BF)


def pair_shift(e):
    row = lax.broadcasted_iota(jnp.int32, (256, 256), 0)
    col = lax.broadcasted_iota(jnp.int32, (256, 256), 1)
    same = (row >> 7) == (col >> 7)
    return jnp.where(same & ((row & 127) == (col & 127) + (e - 1)), 1.0, 0.0).astype(BF)


def pack_weights(weight, second, out):
    for a in range(3):
        for j in range(0, 8, 2):
            pair = jnp.concatenate([weight[9 * a + j], weight[9 * a + j + 1]], axis=1)
            out[a * 64 + j * 8 : a * 64 + j * 8 + 16] = pair
    out[192:208] = jnp.concatenate([weight[8], weight[17]], axis=1)
    out[208:224] = jnp.concatenate([weight[26], jnp.zeros_like(weight[26])], axis=1)
    out[224:1088] = second[...].reshape(864, 128)


def first_rows(pieces, a):
    def stacked(row):
        return jnp.concatenate([piece[row : row + 16] for piece in pieces], axis=0)

    tiles = [stacked(a * 64 + j * 16) for j in range(4)]
    tiles.append(stacked(208 if a == 2 else 192)[:, 64 * (a % 2) : 64 * (a % 2) + 64])
    return jnp.concatenate(tiles, axis=1)


def deal_cot(place, cot, *outs):
    for d, out in enumerate(outs):
        here = (place[1] >> 1) ^ d
        for j in range(4):
            out[j] = cot[4 * here + j]


def sort_cot(place, p0, p1, p2, p3, mine, across):
    core = place[1] & 1
    for d, piece in enumerate((p0, p1, p2, p3)):
        for j in range(2):
            mine[d, j] = piece[2 * core + j]
            across[d, j] = piece[2 - 2 * core + j]


def low_and_high(place, one, two):
    even = place[0] == 0
    two = jnp.where(place[2] == 1, jnp.zeros_like(two), two)
    return jnp.where(even, two, one), jnp.where(even, one, two)


def first_forward(place, own, one, two, packed, across, taps, slope, pooled, weight, edges):
    shifts = [split_shift(e) for e in range(3)]
    pieces = []
    for f in range(8):
        where = place[1] ^ f
        pieces.append(jnp.where((where & 1) == 0, packed[where >> 1], across[where >> 1]))
    parts = [first_rows(pieces, a) for a in range(3)]
    weight[...] = jnp.concatenate(parts, axis=1)
    edges[0] = jnp.concatenate([w[:, 192:] for w in parts], axis=1)
    edges[1] = jnp.concatenate([w[:, :384] for w in parts], axis=1)

    @pl.loop(0, 2)
    def _(s):
        low, high = low_and_high(place, one[s], two[s])
        for depth, cells in enumerate((low, own[s, 0], own[s, 1], high)):
            cells = cells.reshape(256, 256)
            for e in range(3):
                taps[s, depth, :, e * 64 : (e + 1) * 64, :] = (
                    dot(cells, shifts[e]).astype(BF).reshape(4, 64, 256)
                )
        for pair in range(2):
            total = None
            for z in range(2):
                for y in (2 * pair, 2 * pair + 1):
                    first, last = max(y - 1, 0), min(y + 2, 4)
                    size = (last - first) * 192
                    w = weight[...] if size == 576 else edges[y // 3]
                    cells = [taps[s, z + a, first:last].reshape(size, 256) for a in range(3)]
                    pre = dot(w, jnp.concatenate(cells, axis=0))
                    value, rate = gelu_and_slope(pre)
                    slope[s, z, y] = rate
                    total = value if total is None else total + value
            pooled[s, pair] = ((total[:, :128] + total[:, 128:]) * 0.125).astype(BF)


def second_rows(weight, across, k):
    here = slice(224 + 32 * k, 256 + 32 * k)
    return jnp.concatenate(
        [weight[:, here].reshape(128, 128), across[:, here].reshape(128, 128)], axis=0
    )


def forward_rows(weight, across, a, y):
    base = 9 * a + 3 * (1 - y)
    return jnp.concatenate([second_rows(weight, across, base + j) for j in range(6)], axis=1)


def second_start(own, weight, across, taps, begun, turned):
    left, right = pair_shift(0), pair_shift(2)
    for y in range(2):
        cells = jnp.concatenate([own[0, y], own[1, y]], axis=1)
        taps[y, 0:128] = dot(cells, left).astype(BF)
        taps[y, 128:256] = cells
        taps[y, 256:384] = dot(cells, right).astype(BF)
    for y in range(2):
        begun[y] = dot(forward_rows(weight, across, 1, y), taps[...].reshape(768, 256))
    for k in range(27):
        e = k % 3
        turned[k // 3, :, e * 256 : (e + 1) * 256] = second_rows(weight, across, k).T


def second_layer(
    place, one, two, weight, across, cot, cot_across, middle, begun, turned,
    grads, taps, mid, first, second, spread,
):
    even = place[0] == 0
    left, right = pair_shift(0), pair_shift(2)
    for y in range(2):
        low, high = low_and_high(
            place,
            jnp.concatenate([one[0, y], one[1, y]], axis=1),
            jnp.concatenate([two[0, y], two[1, y]], axis=1),
        )
        taps[1, y] = middle[y]
        for a, cells in ((0, low), (2, high)):
            taps[a, y, 0:128] = dot(cells, left).astype(BF)
            taps[a, y, 128:256] = cells
            taps[a, y, 256:384] = dot(cells, right).astype(BF)
    for y in range(2):
        pre = begun[y]
        for a in (0, 2):
            pre = pre + dot(forward_rows(weight, across, a, y), taps[a].reshape(768, 256))
        _, rate = gelu_and_slope(pre)
        pair = [
            jnp.concatenate([c[d, j, y] for c in (cot, cot_across) for d in range(4)], axis=0)
            for j in range(2)
        ]
        grad = (jnp.concatenate(pair, axis=1).astype(F32) * rate).astype(BF)
        grads[y] = grad
        spread[y, 0] = dot(grad, right).astype(BF)
        spread[y, 1] = grad
        spread[y, 2] = dot(grad, left).astype(BF)
    for y in range(2):
        parts = []
        for a in range(3):
            total = None
            for source in range(2):
                w = turned[3 * a + y - source + 1]
                part = dot(w, spread[source].reshape(768, 256))
                total = part if total is None else total + part
            parts.append(total)
        down, mid[y], up = parts
        first[y] = jnp.where(even, up, down).astype(BF)
        second[y] = jnp.where(even, down, up).astype(BF)


def second_weights(grads, taps, mine, across):
    for a in range(3):
        for b in range(3):
            total = None
            for y in range(2):
                row = y + b - 1
                if 0 <= row < 2:
                    part = dot_nt(grads[y], taps[a, row])
                    total = part if total is None else total + part
            total = total.astype(BF)
            for e in range(3):
                k = 9 * a + 3 * b + e
                lanes = slice(e * 128, (e + 1) * 128)
                mine[:, k] = total[:128, lanes].reshape(4, 32, 128)
                across[:, k] = total[128:, lanes].reshape(4, 32, 128)


def add_cores(mine, across, own, *others):
    own[...] = mine[0].astype(F32) + across[0].astype(F32)
    for d, out in enumerate(others):
        out[...] = (mine[d + 1].astype(F32) + across[d + 1].astype(F32)).astype(BF)


def first_weights(place, taps, slope, mid, one, two, out, total):
    inside = place[2] == 0
    total[...] = jnp.zeros_like(total)

    @pl.loop(0, 2)
    def _(s):
        for pair in range(2):
            lanes = pl.ds(pl.multiple_of(s * 128, 128), 128)
            back = (
                mid[pair, :, lanes]
                + one[pair, :, lanes].astype(F32)
                + jnp.where(inside, two[pair, :, lanes].astype(F32), 0.0)
            ) * 0.125
            back = jnp.concatenate([back, back], axis=1)
            inner = [
                jnp.concatenate(
                    [(slope[s, z, 2 * pair + i] * back).astype(BF) for i in range(2)], axis=0
                )
                for z in range(2)
            ]
            inner = jnp.concatenate(inner, axis=1)
            for a in range(3):
                cells = [
                    taps[s, z + a, pair : pair + 3].reshape(576, 256) for z in range(2)
                ]
                part = dot_nt(jnp.concatenate(cells, axis=1), inner)
                if pair == 0:
                    total[a] += part[:, 128:]
                    total[a, 192:576] += part[0:384, :128]
                else:
                    total[a] += part[:, :128]
                    total[a, 0:384] += part[192:576, 128:]

    for a in range(3):
        out[:, a] = total[a].T.astype(BF).reshape(8, 16, 576)


def add_across(own, one, two, three, out):
    out[...] = (
        own[...] + one[...].astype(F32) + two[...].astype(F32) + three[...].astype(F32)
    ).astype(out.dtype)


def pack(first, second, out):
    out[0:864] = second[...].reshape(864, 128)
    for a in range(3):
        total = first[0, a].astype(F32)
        for f in range(1, 8):
            total = total + first[f, a].astype(F32)
        total = total.astype(out.dtype)
        for j in range(4):
            row = 864 + a * 64 + j * 16
            out[row : row + 16] = total[:, j * 128 : (j + 1) * 128]
        row = 1056 + a * 16
        last = total[:, 512:576]
        out[row : row + 16] = jnp.concatenate([last, jnp.zeros_like(last)], axis=1)
    out[1104:1152] = jnp.zeros((48, 128), out.dtype)


def add_up(parts, out):
    total = parts[0].astype(F32)
    for s in range(1, 16):
        total = total + parts[s].astype(F32)
    total = total.astype(out.dtype)
    for s in range(16):
        out[s] = total


def unpack(rows, first, second):
    for k in range(27):
        second[k] = rows[k * 32 : (k + 1) * 32].astype(F32)
    for a in range(3):
        for j in range(9):
            row = 864 + a * 64 + (j // 2) * 16 if j < 8 else 1056 + a * 16
            half = (j % 2) * 64
            first[9 * a + j] = rows[row : row + 16].astype(F32)[:, half : half + 64]


VMEM = pl.BlockSpec(memory_space=pltpu.VMEM)
HBM = pl.BlockSpec(memory_space=pl.ANY)
SMEM = pl.BlockSpec(memory_space=pltpu.SMEM)


def call(kernel, ins, outs, scratch, flops, name, far_in=(), far=(), limit=24):
    shapes = [jax.ShapeDtypeStruct(s, d) for s, d in outs]
    size = sum(x.size * x.dtype.itemsize for x in list(ins) + shapes)
    return pl.pallas_call(
        kernel,
        out_shape=shapes,
        in_specs=[
            SMEM if x.dtype == jnp.int32 else HBM if i in far_in else VMEM for i, x in enumerate(ins)
        ],
        out_specs=[HBM if i in far else VMEM for i in range(len(outs))],
        scratch_shapes=scratch,
        compiler_params=pltpu.CompilerParams(vmem_limit_bytes=limit * 1024 * 1024),
        cost_estimate=pl.CostEstimate(flops=flops, bytes_accessed=size, transcendentals=0),
        name=name,
    )(*ins)


SEND = jnp.bfloat16
LONG = 20_000_000_000


def after(value, *others):
    return lax.optimization_barrier((value,) + others)[0]


def per_device(volume, weight_first, weight_second, cotangent):
    space, filt = lax.axis_index("space"), lax.axis_index("filt")
    ns, nf = lax.axis_size("space"), lax.axis_size("filt")
    parity = space % 2
    edge = ((space == 0) | (space == ns - 1)).astype(jnp.int32)
    place = jnp.stack([parity, filt, edge])
    ones = [(i, i ^ 1) for i in range(ns)]
    twos = [(i, (((i + 1) ^ 1) - 1) % ns) for i in range(ns)]

    by_x = [[(i, i ^ (2 * d)) for i in range(nf)] for d in range(4)]
    by_core = [(i, i ^ 1) for i in range(nf)]

    def face(depth):
        zero = jnp.int32(0)
        cells = lax.dynamic_slice(volume, (2 * filt, depth, zero, zero, zero), (2, 1, 4, 64, 256))
        return cells[:, 0]

    outer, inner = face(1 - parity), face(parity)
    one = lax.ppermute(outer, "space", ones)
    two = lax.ppermute(inner, "space", twos)
    by_sample = lax.all_to_all(cotangent[0], "space", 0, 0, tiled=True)
    (piece,) = call(
        pack_weights, (after(weight_first, outer, inner), weight_second), (((1088, 128), BF),), [], 0, "pack_weights"
    )
    others = [lax.ppermute(piece, "filt", by_x[d]) for d in range(1, 4)]
    own = lax.dynamic_slice_in_dim(after(volume, by_sample), 2 * filt, 2, axis=0)
    weights = jnp.stack([after(w, by_sample, one, two) for w in [piece] + others])
    across = lax.ppermute(weights, "filt", by_core)

    part = ((4, 2, 32, 128), BF)
    pieces = call(deal_cot, (place, by_sample), (part,) * 4, [], 0, "deal_cot")
    pieces = [pieces[0]] + [lax.ppermute(pieces[d], "filt", by_x[d]) for d in range(1, 4)]

    taps, slope, pooled = call(
        first_forward,
        (place, own, one, two, weights, across),
        (((2, 4, 4, 192, 256), BF), ((2, 2, 4, 128, 256), F32), ((2, 2, 128, 128), BF)),
        [
            pltpu.VMEM((128, 1728), BF),
            pltpu.VMEM((2, 128, 1152), BF),
        ],
        LONG,
        "first_forward",
    )
    pool_one = lax.ppermute(pooled, "space", ones)
    pool_two = lax.ppermute(pooled, "space", twos)
    half = ((4, 2, 2, 32, 128), BF)
    cot, cot_across = call(sort_cot, (place, after(pieces[0], pooled), *pieces[1:]), (half, half), [], 0, "sort_cot")
    cot_across = lax.ppermute(cot_across, "filt", by_core)
    middle, begun, turned = call(
        second_start,
        (pooled, weights, across),
        (((2, 384, 256), BF), ((2, 256, 256), F32), ((9, 128, 768), BF)),
        [],
        LONG,
        "second_start",
    )
    grads, taps_second, mid, out_one, out_two = call(
        second_layer,
        (place, pool_one, pool_two, weights, across, cot, cot_across, middle, begun, turned),
        (
            ((2, 256, 256), BF),
            ((3, 2, 384, 256), BF),
            ((2, 128, 256), F32),
            ((2, 128, 256), BF),
            ((2, 128, 256), BF),
        ),
        [pltpu.VMEM((2, 3, 256, 256), BF)],
        2_000_000_000,
        "second_layer",
    )
    back_one = lax.ppermute(out_one, "space", ones)
    back_two = lax.ppermute(out_two, "space", twos)
    mine, across = call(
        second_weights,
        (grads, taps_second),
        (((4, 27, 32, 128), BF), ((4, 27, 32, 128), BF)),
        [],
        900_000_000,
        "second_weights",
    )
    across = lax.ppermute(across, "filt", by_core)
    whole = (27, 32, 128)
    own_second, *others = call(
        add_cores, (mine, across), ((whole, F32),) + ((whole, BF),) * 3, [], 0, "add_cores"
    )
    got_second = [lax.ppermute(others[d - 1], "filt", by_x[d]) for d in range(1, 4)]
    (terms_first,) = call(
        first_weights,
        (place, taps, slope, mid, after(back_one, mine), back_two),
        (((8, 3, 16, 576), BF),),
        [pltpu.VMEM((3, 576, 128), F32)],
        LONG,
        "first_weights",
    )
    got_first = lax.all_to_all(terms_first, "filt", 0, 0, tiled=True)

    (mine_second,) = call(
        add_across, (own_second, *got_second), ((whole, SEND),), [], LONG, "add_across"
    )
    (rows,) = call(pack, (got_first, mine_second), (((1152, 128), SEND),), [], 0, "pack")
    parts = lax.all_to_all(rows.reshape(ns, 72, 128), "space", 0, 0, tiled=True)
    (mine,) = call(add_up, (parts,), (((16, 72, 128), SEND),), [], 0, "add_up")
    rows = lax.all_to_all(mine, "space", 0, 0, tiled=True).reshape(1152, 128)
    return call(
        unpack,
        (rows,),
        (((27, 16, 64), F32), ((27, 32, 128), F32)),
        [],
        0,
        "unpack",
    )


def solution(mesh):
    return jax.shard_map(
        per_device,
        mesh=mesh,
        in_specs=(
            P(None, "space", None, None, None),
            P(None, "filt", None),
            P(None, "filt", None),
            P("space", None, None, "filt", None),
        ),
        out_specs=(P(None, "filt", None), P(None, "filt", None)),
        check_vma=False,
    )
```

```python
import functools

import jax
import jax.numpy as jnp
from jax import lax
from jax.experimental import pallas as pl
from jax.experimental.pallas import tpu as pltpu
from jax.sharding import PartitionSpec as P

BF = jnp.bfloat16
F32 = jnp.float32
ROOT = 0.7978845608028654
CUBE = 0.044715


def dot(a, b):
    return lax.dot_general(a, b, (((1,), (0,)), ((), ())), preferred_element_type=F32)


def dot_nt(a, b):
    return lax.dot_general(a, b, (((1,), (1,)), ((), ())), preferred_element_type=F32)


def dot_tn(a, b):
    return lax.dot_general(a, b, (((0,), (0,)), ((), ())), preferred_element_type=F32)


def gelu_and_slope(v):
    square = v * v
    half = 0.5 + 0.5 * jnp.tanh(v * (ROOT + ROOT * CUBE * square))
    slope = half + (half - half * half) * (v * (2.0 * ROOT + 6.0 * ROOT * CUBE * square))
    return v * half, slope


def split_shift(e):
    row = lax.broadcasted_iota(jnp.int32, (256, 256), 0)
    col = lax.broadcasted_iota(jnp.int32, (256, 256), 1)
    source = 2 * (col & 127) + (col >> 7) + (e - 1)
    return jnp.where(row == source, 1.0, 0.0).astype(BF)


def pair_shift(e):
    row = lax.broadcasted_iota(jnp.int32, (256, 256), 0)
    col = lax.broadcasted_iota(jnp.int32, (256, 256), 1)
    same = (row >> 7) == (col >> 7)
    return jnp.where(same & ((row & 127) == (col & 127) + (e - 1)), 1.0, 0.0).astype(BF)


def pack_weights(weight, second, out):
    for a in range(3):
        for j in range(0, 8, 2):
            pair = jnp.concatenate([weight[9 * a + j], weight[9 * a + j + 1]], axis=1)
            out[a * 64 + j * 8 : a * 64 + j * 8 + 16] = pair
    out[192:208] = jnp.concatenate([weight[8], weight[17]], axis=1)
    out[208:224] = jnp.concatenate([weight[26], jnp.zeros_like(weight[26])], axis=1)
    out[224:1088] = second[...].reshape(864, 128)


def first_rows(pieces, a):
    def stacked(row):
        return jnp.concatenate([piece[row : row + 16] for piece in pieces], axis=0)

    tiles = [stacked(a * 64 + j * 16) for j in range(4)]
    tiles.append(stacked(208 if a == 2 else 192)[:, 64 * (a % 2) : 64 * (a % 2) + 64])
    return jnp.concatenate(tiles, axis=1)


def deal_cot(place, cot, *outs):
    for d, out in enumerate(outs):
        here = (place[1] >> 1) ^ d
        for j in range(4):
            out[j] = cot[4 * here + j]


def sort_cot(place, p0, p1, p2, p3, mine, across):
    core = place[1] & 1
    for d, piece in enumerate((p0, p1, p2, p3)):
        for j in range(2):
            mine[d, j] = piece[2 * core + j]
            across[d, j] = piece[2 - 2 * core + j]


def low_and_high(place, one, two):
    even = place[0] == 0
    two = jnp.where(place[2] == 1, jnp.zeros_like(two), two)
    return jnp.where(even, two, one), jnp.where(even, one, two)


def first_forward(place, own, one, two, packed, across, taps, slope, pooled, weight, edges):
    shifts = [split_shift(e) for e in range(3)]
    pieces = []
    for f in range(8):
        where = place[1] ^ f
        pieces.append(jnp.where((where & 1) == 0, packed[where >> 1], across[where >> 1]))
    parts = [first_rows(pieces, a) for a in range(3)]
    weight[...] = jnp.concatenate(parts, axis=1)
    edges[0] = jnp.concatenate([w[:, 192:] for w in parts], axis=1)
    edges[1] = jnp.concatenate([w[:, :384] for w in parts], axis=1)

    @pl.loop(0, 2)
    def _(s):
        low, high = low_and_high(place, one[s], two[s])
        for depth, cells in enumerate((low, own[s, 0], own[s, 1], high)):
            cells = cells.reshape(256, 256)
            for e in range(3):
                taps[s, depth, :, e * 64 : (e + 1) * 64, :] = (
                    dot(cells, shifts[e]).astype(BF).reshape(4, 64, 256)
                )
        for pair in range(2):
            total = None
            for z in range(2):
                for y in (2 * pair, 2 * pair + 1):
                    first, last = max(y - 1, 0), min(y + 2, 4)
                    size = (last - first) * 192
                    w = weight[...] if size == 576 else edges[y // 3]
                    cells = [taps[s, z + a, first:last].reshape(size, 256) for a in range(3)]
                    pre = dot(w, jnp.concatenate(cells, axis=0))
                    value, rate = gelu_and_slope(pre)
                    slope[s, z, y] = rate
                    total = value if total is None else total + value
            pooled[s, pair] = ((total[:, :128] + total[:, 128:]) * 0.125).astype(BF)


def second_rows(weight, across, k):
    here = slice(224 + 32 * k, 256 + 32 * k)
    return jnp.concatenate(
        [weight[:, here].reshape(128, 128), across[:, here].reshape(128, 128)], axis=0
    )


def forward_rows(weight, across, a, y):
    base = 9 * a + 3 * (1 - y)
    return jnp.concatenate([second_rows(weight, across, base + j) for j in range(6)], axis=1)


def second_start(own, weight, across, taps, begun, turned):
    left, right = pair_shift(0), pair_shift(2)
    for y in range(2):
        cells = jnp.concatenate([own[0, y], own[1, y]], axis=1)
        taps[y, 0:128] = dot(cells, left).astype(BF)
        taps[y, 128:256] = cells
        taps[y, 256:384] = dot(cells, right).astype(BF)
    for y in range(2):
        begun[y] = dot(forward_rows(weight, across, 1, y), taps[...].reshape(768, 256))
    for k in range(27):
        e = k % 3
        turned[k // 3, :, e * 256 : (e + 1) * 256] = second_rows(weight, across, k).T


def second_layer(
    place, one, two, weight, across, cot, cot_across, middle, begun, turned,
    grads, taps, mid, first, second, spread,
):
    even = place[0] == 0
    left, right = pair_shift(0), pair_shift(2)
    for y in range(2):
        low, high = low_and_high(
            place,
            jnp.concatenate([one[0, y], one[1, y]], axis=1),
            jnp.concatenate([two[0, y], two[1, y]], axis=1),
        )
        taps[1, y] = middle[y]
        for a, cells in ((0, low), (2, high)):
            taps[a, y, 0:128] = dot(cells, left).astype(BF)
            taps[a, y, 128:256] = cells
            taps[a, y, 256:384] = dot(cells, right).astype(BF)
    for y in range(2):
        pre = begun[y]
        for a in (0, 2):
            pre = pre + dot(forward_rows(weight, across, a, y), taps[a].reshape(768, 256))
        _, rate = gelu_and_slope(pre)
        pair = [
            jnp.concatenate([c[d, j, y] for c in (cot, cot_across) for d in range(4)], axis=0)
            for j in range(2)
        ]
        grad = (jnp.concatenate(pair, axis=1).astype(F32) * rate).astype(BF)
        grads[y] = grad
        spread[y, 0] = dot(grad, right).astype(BF)
        spread[y, 1] = grad
        spread[y, 2] = dot(grad, left).astype(BF)
    for y in range(2):
        parts = []
        for a in range(3):
            total = None
            for source in range(2):
                w = turned[3 * a + y - source + 1]
                part = dot(w, spread[source].reshape(768, 256))
                total = part if total is None else total + part
            parts.append(total)
        down, mid[y], up = parts
        first[y] = jnp.where(even, up, down).astype(BF)
        second[y] = jnp.where(even, down, up).astype(BF)


def second_weights(grads, taps, mine, across):
    for a in range(3):
        for b in range(3):
            total = None
            for y in range(2):
                row = y + b - 1
                if 0 <= row < 2:
                    part = dot_nt(grads[y], taps[a, row])
                    total = part if total is None else total + part
            total = total.astype(BF)
            for e in range(3):
                k = 9 * a + 3 * b + e
                lanes = slice(e * 128, (e + 1) * 128)
                mine[:, k] = total[:128, lanes].reshape(4, 32, 128)
                across[:, k] = total[128:, lanes].reshape(4, 32, 128)


def add_cores(mine, across, own, *others):
    own[...] = mine[0].astype(F32) + across[0].astype(F32)
    for d, out in enumerate(others):
        out[...] = (mine[d + 1].astype(F32) + across[d + 1].astype(F32)).astype(BF)


def first_weights(place, taps, slope, mid, one, two, out, total):
    inside = place[2] == 0
    total[...] = jnp.zeros_like(total)

    @pl.loop(0, 2)
    def _(s):
        for pair in range(2):
            lanes = pl.ds(pl.multiple_of(s * 128, 128), 128)
            back = (
                mid[pair, :, lanes]
                + one[pair, :, lanes].astype(F32)
                + jnp.where(inside, two[pair, :, lanes].astype(F32), 0.0)
            ) * 0.125
            back = jnp.concatenate([back, back], axis=1)
            inner = [
                jnp.concatenate(
                    [(slope[s, z, 2 * pair + i] * back).astype(BF) for i in range(2)], axis=0
                )
                for z in range(2)
            ]
            inner = jnp.concatenate(inner, axis=1)
            for a in range(3):
                cells = [
                    taps[s, z + a, pair : pair + 3].reshape(576, 256) for z in range(2)
                ]
                part = dot_nt(jnp.concatenate(cells, axis=1), inner)
                if pair == 0:
                    total[a] += part[:, 128:]
                    total[a, 192:576] += part[0:384, :128]
                else:
                    total[a] += part[:, :128]
                    total[a, 0:384] += part[192:576, 128:]

    for a in range(3):
        out[:, a] = total[a].astype(BF).T.reshape(8, 16, 576)


def add_across(own, one, two, three, out):
    out[...] = (
        own[...] + one[...].astype(F32) + two[...].astype(F32) + three[...].astype(F32)
    ).astype(out.dtype)


def pack(first, second, out):
    out[0:864] = second[...].reshape(864, 128)
    for a in range(3):
        total = first[0, a].astype(F32)
        for f in range(1, 8):
            total = total + first[f, a].astype(F32)
        total = total.astype(out.dtype)
        for j in range(4):
            row = 864 + a * 64 + j * 16
            out[row : row + 16] = total[:, j * 128 : (j + 1) * 128]
        row = 1056 + a * 16
        last = total[:, 512:576]
        out[row : row + 16] = jnp.concatenate([last, jnp.zeros_like(last)], axis=1)
    out[1104:1152] = jnp.zeros((48, 128), out.dtype)


def add_up(parts, out):
    total = parts[0].astype(F32)
    for s in range(1, 16):
        total = total + parts[s].astype(F32)
    total = total.astype(out.dtype)
    for s in range(16):
        out[s] = total


def unpack(rows, first, second):
    for k in range(27):
        second[k] = rows[k * 32 : (k + 1) * 32].astype(F32)
    for a in range(3):
        for j in range(9):
            row = 864 + a * 64 + (j // 2) * 16 if j < 8 else 1056 + a * 16
            half = (j % 2) * 64
            first[9 * a + j] = rows[row : row + 16].astype(F32)[:, half : half + 64]


VMEM = pl.BlockSpec(memory_space=pltpu.VMEM)
HBM = pl.BlockSpec(memory_space=pl.ANY)
SMEM = pl.BlockSpec(memory_space=pltpu.SMEM)


def call(kernel, ins, outs, scratch, flops, name, far_in=(), far=(), limit=24):
    shapes = [jax.ShapeDtypeStruct(s, d) for s, d in outs]
    size = sum(x.size * x.dtype.itemsize for x in list(ins) + shapes)
    return pl.pallas_call(
        kernel,
        out_shape=shapes,
        in_specs=[
            SMEM if x.dtype == jnp.int32 else HBM if i in far_in else VMEM for i, x in enumerate(ins)
        ],
        out_specs=[HBM if i in far else VMEM for i in range(len(outs))],
        scratch_shapes=scratch,
        compiler_params=pltpu.CompilerParams(vmem_limit_bytes=limit * 1024 * 1024),
        cost_estimate=pl.CostEstimate(flops=flops, bytes_accessed=size, transcendentals=0),
        name=name,
    )(*ins)


SEND = jnp.bfloat16
LONG = 20_000_000_000


def after(value, *others):
    return lax.optimization_barrier((value,) + others)[0]


def per_device(volume, weight_first, weight_second, cotangent):
    space, filt = lax.axis_index("space"), lax.axis_index("filt")
    ns, nf = lax.axis_size("space"), lax.axis_size("filt")
    parity = space % 2
    edge = ((space == 0) | (space == ns - 1)).astype(jnp.int32)
    place = jnp.stack([parity, filt, edge])
    ones = [(i, i ^ 1) for i in range(ns)]
    twos = [(i, (((i + 1) ^ 1) - 1) % ns) for i in range(ns)]

    by_x = [[(i, i ^ (2 * d)) for i in range(nf)] for d in range(4)]
    by_core = [(i, i ^ 1) for i in range(nf)]

    def face(depth):
        zero = jnp.int32(0)
        cells = lax.dynamic_slice(volume, (2 * filt, depth, zero, zero, zero), (2, 1, 4, 64, 256))
        return cells[:, 0]

    outer, inner = face(1 - parity), face(parity)
    one = lax.ppermute(outer, "space", ones)
    two = lax.ppermute(inner, "space", twos)
    by_sample = lax.all_to_all(cotangent[0], "space", 0, 0, tiled=True)
    (piece,) = call(
        pack_weights, (after(weight_first, outer, inner), weight_second), (((1088, 128), BF),), [], 0, "pack_weights"
    )
    others = [lax.ppermute(piece, "filt", by_x[d]) for d in range(1, 4)]
    own = lax.dynamic_slice_in_dim(after(volume, by_sample), 2 * filt, 2, axis=0)
    weights = jnp.stack([after(w, by_sample, one, two) for w in [piece] + others])
    across = lax.ppermute(weights, "filt", by_core)

    part = ((4, 2, 32, 128), BF)
    pieces = call(deal_cot, (place, by_sample), (part,) * 4, [], 0, "deal_cot")
    pieces = [pieces[0]] + [lax.ppermute(pieces[d], "filt", by_x[d]) for d in range(1, 4)]

    taps, slope, pooled = call(
        first_forward,
        (place, own, one, two, weights, across),
        (((2, 4, 4, 192, 256), BF), ((2, 2, 4, 128, 256), F32), ((2, 2, 128, 128), BF)),
        [
            pltpu.VMEM((128, 1728), BF),
            pltpu.VMEM((2, 128, 1152), BF),
        ],
        LONG,
        "first_forward",
    )
    pool_one = lax.ppermute(pooled, "space", ones)
    pool_two = lax.ppermute(pooled, "space", twos)
    half = ((4, 2, 2, 32, 128), BF)
    cot, cot_across = call(sort_cot, (place, after(pieces[0], pooled), *pieces[1:]), (half, half), [], 0, "sort_cot")
    cot_across = lax.ppermute(cot_across, "filt", by_core)
    middle, begun, turned = call(
        second_start,
        (pooled, weights, across),
        (((2, 384, 256), BF), ((2, 256, 256), F32), ((9, 128, 768), BF)),
        [],
        LONG,
        "second_start",
    )
    grads, taps_second, mid, out_one, out_two = call(
        second_layer,
        (place, pool_one, pool_two, weights, across, cot, cot_across, middle, begun, turned),
        (
            ((2, 256, 256), BF),
            ((3, 2, 384, 256), BF),
            ((2, 128, 256), F32),
            ((2, 128, 256), BF),
            ((2, 128, 256), BF),
        ),
        [pltpu.VMEM((2, 3, 256, 256), BF)],
        2_000_000_000,
        "second_layer",
    )
    back_one = lax.ppermute(out_one, "space", ones)
    back_two = lax.ppermute(out_two, "space", twos)
    mine, across = call(
        second_weights,
        (grads, taps_second),
        (((4, 27, 32, 128), BF), ((4, 27, 32, 128), BF)),
        [],
        900_000_000,
        "second_weights",
    )
    across = lax.ppermute(across, "filt", by_core)
    whole = (27, 32, 128)
    own_second, *others = call(
        add_cores, (mine, across), ((whole, F32),) + ((whole, BF),) * 3, [], 0, "add_cores"
    )
    got_second = [lax.ppermute(others[d - 1], "filt", by_x[d]) for d in range(1, 4)]
    (terms_first,) = call(
        first_weights,
        (place, taps, slope, mid, after(back_one, mine), back_two),
        (((8, 3, 16, 576), BF),),
        [pltpu.VMEM((3, 576, 128), F32)],
        LONG,
        "first_weights",
    )
    got_first = lax.all_to_all(terms_first, "filt", 0, 0, tiled=True)

    (mine_second,) = call(
        add_across, (own_second, *got_second), ((whole, SEND),), [], LONG, "add_across"
    )
    (rows,) = call(pack, (got_first, mine_second), (((1152, 128), SEND),), [], 0, "pack")
    parts = lax.all_to_all(rows.reshape(ns, 72, 128), "space", 0, 0, tiled=True)
    (mine,) = call(add_up, (parts,), (((16, 72, 128), SEND),), [], 0, "add_up")
    rows = lax.all_to_all(mine, "space", 0, 0, tiled=True).reshape(1152, 128)
    return call(
        unpack,
        (rows,),
        (((27, 16, 64), F32), ((27, 32, 128), F32)),
        [],
        0,
        "unpack",
    )


def solution(mesh):
    return jax.shard_map(
        per_device,
        mesh=mesh,
        in_specs=(
            P(None, "space", None, None, None),
            P(None, "filt", None),
            P(None, "filt", None),
            P("space", None, None, "filt", None),
        ),
        out_specs=(P(None, "filt", None), P(None, "filt", None)),
        check_vma=False,
    )
```
